256 devices in a mesh: fr: 2 (over y_lo), gr: 16 (over z, core), gc: 8 (over y_hi, x).
Axes of the slice: x: 4, y: 4 (y_hi: 2, y_lo: 2; y = y_hi * 2 + y_lo), z: 8, core: 2. Of those that a mesh axis runs over, the one named last changes fastest.
Arguments:
- front: bfloat16 [6, 8192, 8192], P('fr', 'gr', 'gc'), parts along dimension 0
- omega: bfloat16 [6, 8192, 256], P('fr', 'gc'), parts along dimension 0, may hold values from -6 to 6
- child_sketch: bfloat16 [6, 2, 2048, 256], P('fr', None, ('gr', 'gc')), parts along dimension 0, may hold values from -6 to 6
- child_map: int32 [6, 2, 2048], P('fr', None, ('gr', 'gc')), parts along dimension 0, may hold values from 0 to 8191, as said below
- picks: int32 [6, 16, 128], P('fr'), parts along dimension 0, may hold values from 0 to 511, as said below
Outputs:
- sketch: float32 [6, 8192, 256], P('fr', 'gr', 'gc'), parts along dimension 0
- basis: float32 [6, 8192, 128], P('fr', 'gr'), parts along dimension 0
- coupling: bfloat16 [6, 2048, 2048], P('fr', 'gr', 'gc'), parts along dimension 0
The draws below stay inside these ranges and needn't reach their ends.
There are 2 independent parts, one for each index of `fr`. The reference program is written for one: setup_inputs(seed, part) draws one part's arguments, and reference() takes and returns one part's arrays. A program takes and returns all parts, laid end to end along the dimension named above; each array names one. Nothing has to cross between parts.
Inputs may be any that keep to these rules, and one draw needn't show every extreme that they name: `child_map`: within each child the 2048 entries are distinct. Within each block the 128 picks are distinct.
All inputs are finite; a program needn't handle non-finite values.
Results may differ from the reference program's by a relative error of at most 0.0004.
Values may be sent and summed in bfloat16 or wider, within the bound.
A program may use at most 64 MiB of HBM per device.

```python
import jax
import jax.numpy as jnp
from jax import lax

F = 8192
R = 256
CU = 2048
K = 128
NCH = 2
NF = 3
NB = 16
LB = 512


def distinct_rows(key, total, taken):
    order = jax.random.permutation(key, total)[:taken]
    return (order + (total - 1 - order[0])) % total


def make_child_map(key):
    key = jax.random.fold_in(key, 11)
    keys = jax.random.split(key, NF * NCH)
    rows = jax.vmap(lambda one_key: distinct_rows(one_key, F, CU))(keys)
    return rows.reshape(NF, NCH, CU).astype(jnp.int32)


def draw_child_map(key, part):
    return make_child_map(key)


def draw_picks(key, part):
    key = jax.random.fold_in(key, 23)
    keys = jax.random.split(key, NF * NB)
    rows = jax.vmap(lambda one_key: distinct_rows(one_key, LB, K))(keys)
    return rows.reshape(NF, NB, K).astype(jnp.int32)


def row_scales(key, growth):
    position = jnp.arange(F, dtype=jnp.float32) / F
    rough = jnp.exp(jax.random.uniform(key, (NF, F, 1), jnp.float32, 0.0, jnp.log(2.0)))
    return jnp.exp(jnp.log(growth) * position)[None, :, None] * rough


def make_front(key, growth):
    key = jax.random.fold_in(key, 37)
    scale_key, value_key = jax.random.split(key)
    scales = row_scales(scale_key, growth)
    bell_values = jnp.clip(jax.random.normal(value_key, (NF, F, F), jnp.float32), -6.0, 6.0)
    values = bell_values
    return (values * scales * F ** (-0.5)).astype(jnp.bfloat16)


def make_omega(key):
    key = jax.random.fold_in(key, 41)
    values = jnp.clip(jax.random.normal(key, (NF, F, R), jnp.float32), -6.0, 6.0)
    return values.astype(jnp.bfloat16)


def draw_front(key, part):
    return make_front(key, 10.0)


def draw_omega(key, part):
    return make_omega(key)


def draw_child_sketch(key, part):
    front = make_front(key, 10.0)
    omega = make_omega(key)
    child_map = make_child_map(key)
    key = jax.random.fold_in(key, 53)
    block_ids = jnp.arange(F) // LB
    off_diag = block_ids[:, None] != block_ids[None, :]
    masked = jnp.where(off_diag[None], front.astype(jnp.float32), 0.0)
    parent = jnp.einsum('frk,fkc->frc', masked, omega.astype(jnp.float32), precision=lax.Precision.HIGHEST)
    landed = jax.vmap(lambda whole, rows: whole[rows])(parent, child_map)
    noise = jnp.clip(jax.random.normal(key, (NF, NCH, CU, R), jnp.float32), -6.0, 6.0)
    return jnp.clip(0.5 * landed + noise, -6.0, 6.0).astype(jnp.bfloat16)


def setup_inputs(seed: int = 0, part: int = 0) -> dict:
    arg_keys = jax.random.split(jax.random.key(seed), 6)
    own_keys = jax.random.split(jax.random.fold_in(arg_keys[5], part), 6)
    front = draw_front(jax.random.fold_in(jax.random.fold_in(arg_keys[5], part), 71), part)
    omega = draw_omega(jax.random.fold_in(jax.random.fold_in(arg_keys[5], part), 71), part)
    child_sketch = draw_child_sketch(jax.random.fold_in(jax.random.fold_in(arg_keys[5], part), 71), part)
    child_map = draw_child_map(jax.random.fold_in(jax.random.fold_in(arg_keys[5], part), 71), part)
    picks = draw_picks(jax.random.fold_in(jax.random.fold_in(arg_keys[5], part), 71), part)
    return {"front": front, "omega": omega, "child_sketch": child_sketch, "child_map": child_map, "picks": picks}


def solve_block(factor, rhs):
    return jax.scipy.linalg.cho_solve((factor, True), rhs)

def reference(front, omega, child_sketch, child_map, picks):
    block_ids = jnp.arange(F) // LB
    off_diag = block_ids[:, None] != block_ids[None, :]
    sketches = []
    bases = []
    couplings = []
    for front_id in range(NF):
        masked = jnp.where(off_diag, front[front_id], jnp.zeros((), jnp.bfloat16))
        summed = jnp.dot(masked.astype(jnp.float32), omega[front_id].astype(jnp.float32), preferred_element_type=jnp.float32)
        for child_id in range(NCH):
            summed = summed.at[child_map[front_id, child_id]].add(child_sketch[front_id, child_id].astype(jnp.float32))
        level = 0.5 * jnp.sum(summed * summed) / F + 1e-05
        blocked = summed.reshape(NB, LB, R)
        skeleton = jnp.take_along_axis(blocked, picks[front_id][:, :, None], axis=1)
        gram = jnp.einsum('bkr,bmr->bkm', skeleton, skeleton, precision=lax.Precision.HIGHEST)
        gram = gram + level * jnp.eye(K, dtype=jnp.float32)[None]
        cross = jnp.einsum('blr,bkr->blk', blocked, skeleton, precision=lax.Precision.HIGHEST)
        factor = jnp.linalg.cholesky(gram)
        solved = jax.vmap(solve_block)(factor, jnp.transpose(cross, (0, 2, 1)))
        bases.append(jnp.transpose(solved, (0, 2, 1)).reshape(F, K))
        sketches.append(summed)
        global_rows = ((jnp.arange(NB) * LB)[:, None] + picks[front_id]).reshape(NB * K).astype(jnp.int32)
        couplings.append(front[front_id][global_rows][:, global_rows])
    return (jnp.stack(sketches), jnp.stack(bases), jnp.stack(couplings))
```

```python
import functools
import math

import jax
import jax.numpy as jnp
from jax import lax
from jax.experimental import pallas as pl
from jax.experimental.pallas import tpu as pltpu
from jax.sharding import PartitionSpec as P

MESH = pl.DeviceIdType.MESH
F32 = jnp.float32
BF16 = jnp.bfloat16
I32 = jnp.int32
NF = 3
LB = 512
R = 256
K = 128
NC = 8
NZ = 8
CH = LB // NC
MSG = CH + 8
STEP = math.log(2.0) / 8.0
TOP = 32760.0
SMALLEST = 2.0**-110


def dot(a, b):
    return lax.dot_general(a, b, (((1,), (0,)), ((), ())), preferred_element_type=F32)


def dot_t(a, b):
    return lax.dot_general(a, b, (((1,), (1,)), ((), ())), preferred_element_type=F32)


def split(x):
    hi = x.astype(BF16)
    return hi, (x - hi.astype(F32)).astype(BF16)


def diagonal(rows, columns):
    shape = (rows, columns)
    return lax.broadcasted_iota(I32, shape, 0) == lax.broadcasted_iota(I32, shape, 1)


def encode(x):
    top = jnp.maximum(jnp.max(jnp.abs(x), axis=1, keepdims=True), SMALLEST)
    level = jnp.ceil(jnp.log(top) * (1.0 / STEP))
    q = jnp.round(x * (jnp.exp(level * -STEP) * TOP)).astype(I32)
    packed = (q[:, : R // 2] << 16) | (q[:, R // 2 :] & 0xFFFF)
    levels = jnp.sum(jnp.where(diagonal(CH, 128), level, 0.0), axis=0, keepdims=True)
    return packed, jnp.broadcast_to(levels.astype(I32), (8, 128))


def decode(packed, levels):
    level = jnp.sum(jnp.where(diagonal(CH, 128), levels.astype(F32), 0.0), axis=1, keepdims=True)
    scale = jnp.exp(level * STEP) * (1.0 / TOP)
    first = (packed >> 16).astype(F32) * scale
    second = ((packed << 16) >> 16).astype(F32) * scale
    return first, second


def exchange_kernel(
    front_hbm, omega_hbm, child_hbm, map_ref, picks_ref,
    sketch_ref, energy_ref, coupling_ref,
    front, omega, child_all, maps, partial, rs_out, rs_in, ag_in, en1, en2,
    load_sem, child_s, child_r, map_s, map_r, core_s, core_r, rs_s, rs_r, ag_s, ag_r, e1_s, e1_r, e2_s, e2_r,
):
    fr = lax.axis_index("fr")
    gr = lax.axis_index("gr")
    gc = lax.axis_index("gc")
    z = gr // 2
    core = gr % 2

    def z_peer(d):
        zz = lax.rem(z + d + NZ, NZ)
        return zz, (fr, zz * 2 + core, gc)

    def c_peer(d):
        cc = lax.rem(gc + d + NC, NC)
        return cc, (fr, gr, cc)

    def g_peer(d):
        gg = lax.rem(gr + d + 16, 16)
        return gg, (fr, gg, gc)

    partner = (fr, z * 2 + (1 - core), gc)

    loads = []
    own_child = []
    for f in range(NF):
        own_child.append(pltpu.make_async_copy(child_hbm.at[f], child_all.at[f, core, z], load_sem.at[f]))
        own_child[f].start()
    own_map = pltpu.make_async_copy(map_ref, maps.at[core, z], load_sem.at[9])
    own_map.start()
    for f in range(NF):
        a = pltpu.make_async_copy(front_hbm.at[f], front.at[f], load_sem.at[3 + f])
        b = pltpu.make_async_copy(omega_hbm.at[f], omega.at[f], load_sem.at[6 + f])
        b.start()
        a.start()
        loads.append((a, b))

    barrier = pltpu.get_barrier_semaphore()
    for d in range(1, 16):
        pl.semaphore_signal(barrier, inc=1, device_id=g_peer(d)[1], device_id_type=MESH)
    for d in range(1, NC):
        pl.semaphore_signal(barrier, inc=1, device_id=c_peer(d)[1], device_id_type=MESH)
    pl.semaphore_wait(barrier, 22)

    sends = []

    def send(src, dst, s, r, device):
        copy = pltpu.make_async_remote_copy(
            src_ref=src, dst_ref=dst, send_sem=s, recv_sem=r, device_id=device, device_id_type=MESH
        )
        copy.start()
        sends.append(copy)

    def arrive(dst, s, r, device):
        pltpu.make_async_remote_copy(
            src_ref=dst, dst_ref=dst, send_sem=s, recv_sem=r, device_id=device, device_id_type=MESH
        ).wait_recv()

    for d in (4, 3, 5, 2, 6, 1, 7):
        device = z_peer(d)[1]
        send(map_ref, maps.at[core, z], map_s.at[d - 1], map_r.at[z], device)
    for f in range(NF):
        for d in (4, 3, 5, 2, 6, 1, 7):
            device = z_peer(d)[1]
            send(child_hbm.at[f], child_all.at[f, core, z], child_s.at[f, d - 1], child_r.at[f, z], device)

    for f in range(NF):
        loads[f][0].wait()
        loads[f][1].wait()
        for half in range(2):
            rows = pl.ds(half * LB, LB)
            off = gr != 2 * gc + half
            omega[f, rows, :] = jnp.where(off, omega[f, rows, :], jnp.zeros((), BF16))
        for r in range(4):
            rows = pl.ds(r * 128, 128)
            partial[f, rows, :] = dot(front[f, rows, :], omega[f])

    own_map.wait()
    for d in range(1, NZ):
        zz, device = z_peer(-d)
        arrive(maps.at[core, zz], map_s.at[d - 1], map_r.at[zz], device)
    send(maps.at[core], maps.at[core], map_s.at[7], map_r.at[8], partner)

    targets = None
    for f in range(NF):
        own_child[f].wait()
        for d in range(1, NZ):
            zz, device = z_peer(-d)
            arrive(child_all.at[f, core, zz], child_s.at[f, d - 1], child_r.at[f, zz], device)
        send(child_all.at[f, core], child_all.at[f, core], core_s.at[f], core_r.at[f], partner)

        picked = picks_ref[f, pl.ds(gr, 1), :]
        down = jnp.transpose(jnp.broadcast_to(picked, (K, K)))
        lanes = lax.broadcasted_iota(I32, (K, K), 1)
        pick_rows = jnp.concatenate([(down == lanes + 128 * t).astype(BF16) for t in range(4)], axis=1)
        mine = dot(pick_rows, front[f]).astype(BF16)
        for half in range(2):
            wanted = picks_ref[f, pl.ds(2 * gc + half, 1), :]
            pick_columns = (lax.broadcasted_iota(I32, (LB, K), 0) == wanted).astype(BF16)
            coupling_ref[f, :, half * K : (half + 1) * K] = dot(
                mine[:, half * LB : (half + 1) * LB], pick_columns
            ).astype(BF16)

        if targets is None:
            arrive(maps.at[1 - core], map_s.at[7], map_r.at[8], partner)
            targets = []
            for k in range(2):
                for h in range(2):
                    tile = maps[k, 4 * h]
                    for t in range(1, 4):
                        tile = tile + maps[k, 4 * h + t]
                    targets.append(tile - gr * LB)
        arrive(child_all.at[f, 1 - core], core_s.at[f], core_r.at[f], partner)

        for c in range(NC):
            rows = lax.broadcasted_iota(I32, (CH, 128), 0) + c * CH
            total = partial[f, c * CH : (c + 1) * CH, :]
            hits = jnp.concatenate([(rows == tile[f : f + 1, :]).astype(BF16) for tile in targets], axis=1)
            total = total + dot(hits, child_all[f].reshape(2 * NZ * 32, R))
            partial[f, c * CH : (c + 1) * CH, :] = total
            packed, levels = encode(total)
            rs_out[f, c, 0:CH, :] = packed
            rs_out[f, c, CH:MSG, :] = levels
        for d in (5, 6, 7, 2, 4, 1, 3):
            cc, device = c_peer(d)
            send(rs_out.at[f, cc], rs_in.at[f, gc], rs_s.at[f, d - 1], rs_r.at[f, gc], device)

    energies = []
    for f in range(NF):
        own = partial[f, pl.ds(gc * CH, CH), :]
        first, second = own[:, :128], own[:, 128:]
        for d in range(1, NC):
            cc, device = c_peer(-d)
            arrive(rs_in.at[f, cc], rs_s.at[f, d - 1], rs_r.at[f, cc], device)
            a, b = decode(rs_in[f, cc, 0:CH, :], rs_in[f, cc, CH : CH + 1, :])
            first, second = first + a, second + b
        total = jnp.concatenate([first, second], axis=1)
        packed, levels = encode(total)
        ag_in[f, gc, 0:CH, :] = packed
        ag_in[f, gc, CH:MSG, :] = levels
        for d in (5, 6, 7, 2, 4, 1, 3):
            cc, device = c_peer(d)
            send(ag_in.at[f, gc], ag_in.at[f, gc], ag_s.at[f, d - 1], ag_r.at[f, gc], device)
        energies.append(jnp.sum(first * first + second * second, axis=0, keepdims=True))

    en1[gr] = jnp.concatenate(energies + [jnp.zeros((8 - NF, 128), F32)], axis=0)
    for d in range(1, 16):
        send(en1.at[gr], en1.at[gr], e1_s.at[d - 1], e1_r.at[gr], g_peer(d)[1])
    for d in range(1, 16):
        gg, device = g_peer(-d)
        arrive(en1.at[gg], e1_s.at[d - 1], e1_r.at[gg], device)
    en2[gc] = functools.reduce(lambda a, b: a + b, [en1[g] for g in range(16)])
    for d in range(1, NC):
        send(en2.at[gc], en2.at[gc], e2_s.at[d - 1], e2_r.at[gc], c_peer(d)[1])

    for f in range(NF):
        for d in range(1, NC):
            cc, device = c_peer(-d)
            arrive(ag_in.at[f, cc], ag_s.at[f, d - 1], ag_r.at[f, cc], device)
        for c in range(NC):
            a, b = decode(ag_in[f, c, 0:CH, :], ag_in[f, c, CH : CH + 1, :])
            sketch_ref[f, c * CH : (c + 1) * CH, 0:128] = a
            sketch_ref[f, c * CH : (c + 1) * CH, 128:256] = b

    for d in range(1, NC):
        cc, device = c_peer(-d)
        arrive(en2.at[cc], e2_s.at[d - 1], e2_r.at[cc], device)
    energy_ref[...] = functools.reduce(lambda a, b: a + b, [en2[c] for c in range(NC)])
    for copy in sends:
        copy.wait_send()


def mm3(a, b):
    a0, a1 = split(a)
    b0, b1 = split(b)
    return dot(a0, b0) + (dot(a0, b1) + dot(a1, b0))


def high(a, b):
    return lax.dot_general(
        a, b, (((1,), (0,)), ((), ())), preferred_element_type=F32, precision=lax.Precision.HIGHEST
    )


def solve_kernel(sketch_ref, energy_ref, picks_ref, basis_ref, own_ref):
    gr = lax.axis_index("gr")
    gc = lax.axis_index("gc")
    eye = diagonal(K, K)
    grams = []
    crosses = []
    states = []
    for f in range(NF):
        s0, s1 = split(sketch_ref[f])
        picked = picks_ref[f, pl.ds(gr, 1), :]
        down = jnp.transpose(jnp.broadcast_to(picked, (K, K)))
        lanes = lax.broadcasted_iota(I32, (K, K), 1)
        pick_rows = jnp.concatenate([(down == lanes + 128 * t).astype(BF16) for t in range(4)], axis=1)
        k0 = dot(pick_rows, s0).astype(BF16)
        k1 = dot(pick_rows, s1).astype(BF16)
        gram = dot_t(k0, k0) + (dot_t(k0, k1) + dot_t(k1, k0))
        crosses.append(dot_t(s0, k0) + (dot_t(s0, k1) + dot_t(s1, k0)))
        energy = jnp.sum(energy_ref[f : f + 1, :], axis=1, keepdims=True)
        level = 0.5 * energy / 8192.0 + 1e-05
        gram = gram + jnp.where(eye, level, 0.0)
        bound = jnp.max(jnp.sum(jnp.abs(gram), axis=1, keepdims=True), axis=0, keepdims=True)
        trace = jnp.sum(
            jnp.sum(jnp.where(eye, gram, 0.0), axis=1, keepdims=True), axis=0, keepdims=True
        )
        top = jnp.minimum(bound, trace)
        c = 2.0 / (level + top)
        low = level * c
        gain = low * (2.0 - low)
        s = 2.0 / (1.0 + gain)
        x = jnp.where(eye, 2.0 * s * c, 0.0) - (s * c * c) * gram
        grams.append(gram)
        states.append((x, s * gain))
    for step in range(11):
        mm = mm3 if step < 9 else high
        for f in range(NF):
            x, low = states[f]
            gain = low * (2.0 - low)
            s = 2.0 / (1.0 + gain)
            y = jnp.where(eye, 2.0 * s, 0.0) - s * mm(grams[f], x)
            states[f] = (mm(x, y), s * gain)
    for f in range(NF):
        basis_ref[f] = mm3(crosses[f], states[f][0])
        half = jnp.where(gc < 4, sketch_ref[f, :, 0:128], sketch_ref[f, :, 128:256])
        own_ref[f] = pltpu.roll(half, lax.rem(4 - lax.rem(gc, 4), 4) * 32, 1)[:, 0:32]


def body(front, omega, child_sketch, child_map, picks):
    gr = lax.axis_index("gr")
    z = gr // 2
    child = child_sketch.reshape(NF, 32, R)
    own_map = jnp.pad(jnp.tile(child_map.reshape(NF, 32), (1, 4)), ((0, 8 - NF), (0, 0)))
    lane = lax.broadcasted_iota(I32, (8, 128), 1)
    own_map = jnp.where(lane // 32 == z % 4, own_map, 0)
    any_space = pl.BlockSpec(memory_space=pl.ANY)
    vmem = pl.BlockSpec(memory_space=pltpu.VMEM)
    dma = pltpu.SemaphoreType.DMA
    sketch, energy, coupling = pl.pallas_call(
        exchange_kernel,
        out_shape=(
            jax.ShapeDtypeStruct((NF, LB, R), F32),
            jax.ShapeDtypeStruct((8, 128), F32),
            jax.ShapeDtypeStruct((NF, K, 2 * K), BF16),
        ),
        in_specs=[any_space, any_space, any_space, vmem, vmem],
        out_specs=(vmem, vmem, vmem),
        scratch_shapes=[
            pltpu.VMEM((NF, LB, 1024), BF16),
            pltpu.VMEM((NF, 1024, R), BF16),
            pltpu.VMEM((NF, 2, NZ, 32, R), BF16),
            pltpu.VMEM((2, NZ, 8, 128), I32),
            pltpu.VMEM((NF, LB, R), F32),
            pltpu.VMEM((NF, NC, MSG, 128), I32),
            pltpu.VMEM((NF, NC, MSG, 128), I32),
            pltpu.VMEM((NF, NC, MSG, 128), I32),
            pltpu.VMEM((16, 8, 128), F32),
            pltpu.VMEM((NC, 8, 128), F32),
            dma((10,)),
            dma((NF, 7)), dma((NF, NZ)),
            dma((8,)), dma((9,)),
            dma((NF,)), dma((NF,)),
            dma((NF, 7)), dma((NF, NC)),
            dma((NF, 7)), dma((NF, NC)),
            dma((15,)), dma((16,)),
            dma((7,)), dma((NC,)),
        ],
        compiler_params=pltpu.CompilerParams(
            collective_id=0, has_side_effects=True, vmem_limit_bytes=48 * 2**20
        ),
        name="exchange",
    )(front, omega, child, own_map, picks)
    basis, own = pl.pallas_call(
        solve_kernel,
        out_shape=(
            jax.ShapeDtypeStruct((NF, LB, K), F32),
            jax.ShapeDtypeStruct((NF, LB, 32), F32),
        ),
        in_specs=[vmem, vmem, vmem],
        out_specs=(vmem, vmem),
        compiler_params=pltpu.CompilerParams(vmem_limit_bytes=48 * 2**20),
        name="solve",
    )(sketch, energy, picks)
    return own, basis, coupling


def solution(mesh):
    return jax.shard_map(
        body,
        mesh=mesh,
        in_specs=(
            P("fr", "gr", "gc"),
            P("fr", "gc", None),
            P("fr", None, ("gr", "gc"), None),
            P("fr", None, ("gr", "gc")),
            P("fr", None, None),
        ),
        out_specs=(P("fr", "gr", "gc"), P("fr", "gr", None), P("fr", "gr", "gc")),
        check_vma=False,
    )
```

```python
import functools
import math

import jax
import jax.numpy as jnp
from jax import lax
from jax.experimental import pallas as pl
from jax.experimental.pallas import tpu as pltpu
from jax.sharding import PartitionSpec as P

MESH = pl.DeviceIdType.MESH
F32 = jnp.float32
BF16 = jnp.bfloat16
I32 = jnp.int32
NF = 3
LB = 512
R = 256
K = 128
NC = 8
NZ = 8
CH = LB // NC
MSG = CH + 1
SLOT = CH + 8
STEP = math.log(2.0) / 8.0
TOP = 32760.0
SMALLEST = 2.0**-110
MOST = 14
NEAR = 3e-3


def dot(a, b):
    return lax.dot_general(a, b, (((1,), (0,)), ((), ())), preferred_element_type=F32)


def dot_t(a, b):
    return lax.dot_general(a, b, (((1,), (1,)), ((), ())), preferred_element_type=F32)


def split(x):
    hi = x.astype(BF16)
    return hi, (x - hi.astype(F32)).astype(BF16)


def diagonal(rows, columns):
    shape = (rows, columns)
    return lax.broadcasted_iota(I32, shape, 0) == lax.broadcasted_iota(I32, shape, 1)


def encode(x):
    top = jnp.maximum(jnp.max(jnp.abs(x), axis=1, keepdims=True), SMALLEST)
    level = jnp.ceil(jnp.log(top) * (1.0 / STEP))
    q = jnp.round(x * (jnp.exp(level * -STEP) * TOP)).astype(I32)
    packed = (q[:, : R // 2] << 16) | (q[:, R // 2 :] & 0xFFFF)
    levels = jnp.sum(jnp.where(diagonal(CH, 128), level, 0.0), axis=0, keepdims=True)
    return packed, levels.astype(I32)


def decode(packed, levels):
    level = jnp.sum(jnp.where(diagonal(CH, 128), levels.astype(F32), 0.0), axis=1, keepdims=True)
    scale = jnp.exp(level * STEP) * (1.0 / TOP)
    first = (packed >> 16).astype(F32) * scale
    second = ((packed << 16) >> 16).astype(F32) * scale
    return first, second


def exchange_kernel(
    front_hbm, omega_hbm, child_hbm, map_hbm, picks_hbm,
    gram_ref, cross_ref, own_ref, energy_ref, coupling_ref,
    front, omega, child_all, maps, map_in, picks_ref, partial, rs_out, rs_in, ag_in, en1, en2, pick_rows, high_part, low_part, own_half,
    load_sem, child_s, child_r, map_s, map_r, core_s, core_r, rs_s, rs_r, ag_s, ag_r, e1_s, e1_r, e2_s, e2_r,
):
    fr = lax.axis_index("fr")
    gr = lax.axis_index("gr")
    gc = lax.axis_index("gc")
    z = gr // 2
    core = gr % 2

    def z_peer(d):
        zz = lax.rem(z + d + NZ, NZ)
        return zz, (fr, zz * 2 + core, gc)

    def c_peer(d):
        cc = lax.rem(gc + d + NC, NC)
        return cc, (fr, gr, cc)

    def g_peer(d):
        gg = lax.rem(gr + d + 16, 16)
        return gg, (fr, gg, gc)

    partner = (fr, z * 2 + (1 - core), gc)

    loads = []
    own_child = []
    for f in range(NF):
        own_child.append(pltpu.make_async_copy(child_hbm.at[f], child_all.at[f, core, z], load_sem.at[f]))
        own_child[f].start()
    own_map = pltpu.make_async_copy(map_hbm, map_in, load_sem.at[9])
    own_map.start()
    for f in range(NF):
        a = pltpu.make_async_copy(front_hbm.at[f], front.at[f], load_sem.at[3 + f])
        b = pltpu.make_async_copy(omega_hbm.at[f], omega.at[f], load_sem.at[6 + f])
        b.start()
        a.start()
        loads.append((a, b))

    picks_load = pltpu.make_async_copy(picks_hbm, picks_ref, load_sem.at[10])
    picks_load.start()

    barrier = pltpu.get_barrier_semaphore()
    for d in range(1, 16):
        pl.semaphore_signal(barrier, inc=1, device_id=g_peer(d)[1], device_id_type=MESH)
    for d in range(1, NC):
        pl.semaphore_signal(barrier, inc=1, device_id=c_peer(d)[1], device_id_type=MESH)
    own_map.wait()
    lane = lax.broadcasted_iota(I32, (1, 128), 1)
    tile = []
    for f in range(NF):
        both = jnp.concatenate([map_in[f, 0:1, :], map_in[f, 1:2, :]] * 4, axis=1)
        tile.append(jnp.where(lane // 32 == z % 4, both, 0))
    maps[core, z] = jnp.concatenate(tile + [jnp.zeros((8 - NF, 128), I32)], axis=0)
    pl.semaphore_wait(barrier, 22)

    sends = []

    def send(src, dst, s, r, device):
        copy = pltpu.make_async_remote_copy(
            src_ref=src, dst_ref=dst, send_sem=s, recv_sem=r, device_id=device, device_id_type=MESH
        )
        copy.start()
        sends.append(copy)

    def arrive(dst, s, r, device):
        pltpu.make_async_remote_copy(
            src_ref=dst, dst_ref=dst, send_sem=s, recv_sem=r, device_id=device, device_id_type=MESH
        ).wait_recv()

    for d in (4, 3, 5, 2, 6, 1, 7):
        device = z_peer(d)[1]
        send(maps.at[core, z], maps.at[core, z], map_s.at[d - 1], map_r.at[z], device)

    def send_children(f):
        if f > 0:
            for copy in paced:
                copy.wait_send()
            paced.clear()
        own_child[f].wait()
        for d in (4, 3, 5, 2, 6, 1, 7):
            src = child_all.at[f, core, z]
            copy = pltpu.make_async_remote_copy(
                src_ref=src, dst_ref=src, send_sem=child_s.at[f, d - 1], recv_sem=child_r.at[f, z],
                device_id=z_peer(d)[1], device_id_type=MESH,
            )
            copy.start()
            paced.append(copy)

    paced = []
    send_children(0)

    for f in range(NF):
        loads[f][0].wait()
        loads[f][1].wait()
        for half in range(2):
            rows = pl.ds(half * LB, LB)
            off = gr != 2 * gc + half
            omega[f, rows, :] = jnp.where(off, omega[f, rows, :], jnp.zeros((), BF16))
        for r in range(4):
            rows = pl.ds(r * 128, 128)
            partial[f, rows, :] = dot(front[f, rows, :], omega[f])
        if f == 1:
            send_children(1)

    for d in range(1, NZ):
        zz, device = z_peer(-d)
        arrive(maps.at[core, zz], map_s.at[d - 1], map_r.at[zz], device)
    send(maps.at[core], maps.at[core], map_s.at[7], map_r.at[8], partner)

    targets = None
    picks_load.wait()
    for f in range(NF):
        for d in range(1, NZ):
            zz, device = z_peer(-d)
            arrive(child_all.at[f, core, zz], child_s.at[f, d - 1], child_r.at[f, zz], device)
        send(child_all.at[f, core], child_all.at[f, core], core_s.at[f], core_r.at[f], partner)
        if f == 0:
            send_children(2)

        picked = picks_ref[f, pl.ds(gr, 1), :]
        down = jnp.transpose(jnp.broadcast_to(picked, (K, K)))
        lanes = lax.broadcasted_iota(I32, (K, K), 1)
        pick_rows[f] = jnp.concatenate([(down == lanes + 128 * t).astype(BF16) for t in range(4)], axis=1)
        mine = dot(pick_rows[f], front[f]).astype(BF16)
        for half in range(2):
            wanted = picks_ref[f, pl.ds(2 * gc + half, 1), :]
            pick_columns = (lax.broadcasted_iota(I32, (LB, K), 0) == wanted).astype(BF16)
            coupling_ref[f, :, half * K : (half + 1) * K] = dot(
                mine[:, half * LB : (half + 1) * LB], pick_columns
            ).astype(BF16)

        if targets is None:
            arrive(maps.at[1 - core], map_s.at[7], map_r.at[8], partner)
            targets = []
            for k in range(2):
                for h in range(2):
                    tile = maps[k, 4 * h]
                    for t in range(1, 4):
                        tile = tile + maps[k, 4 * h + t]
                    targets.append(tile - gr * LB)
        arrive(child_all.at[f, 1 - core], core_s.at[f], core_r.at[f], partner)

        for c in range(NC):
            rows = lax.broadcasted_iota(I32, (CH, 128), 0) + c * CH
            total = partial[f, c * CH : (c + 1) * CH, :]
            hits = jnp.concatenate([(rows == tile[f : f + 1, :]).astype(BF16) for tile in targets], axis=1)
            total = total + dot(hits, child_all[f].reshape(2 * NZ * 32, R))
            partial[f, c * CH : (c + 1) * CH, :] = total
            packed, levels = encode(total)
            rs_out[f, c, 0:CH, :] = packed
            rs_out[f, c, CH:MSG, :] = levels
        for d in (5, 6, 7, 2, 4, 1, 3):
            cc, device = c_peer(d)
            send(rs_out.at[f, cc, 0:MSG, :], rs_in.at[f, gc, 0:MSG, :], rs_s.at[f, d - 1], rs_r.at[f, gc], device)

    energies = []
    for f in range(NF):
        own = partial[f, pl.ds(gc * CH, CH), :]
        first, second = own[:, :128], own[:, 128:]
        for d in range(1, NC):
            cc, device = c_peer(-d)
            arrive(rs_in.at[f, cc, 0:MSG, :], rs_s.at[f, d - 1], rs_r.at[f, cc], device)
            a, b = decode(rs_in[f, cc, 0:CH, :], rs_in[f, cc, CH : CH + 1, :])
            first, second = first + a, second + b
        total = jnp.concatenate([first, second], axis=1)
        packed, levels = encode(total)
        ag_in[f, gc, 0:CH, :] = packed
        ag_in[f, gc, CH:MSG, :] = levels
        for d in (5, 6, 7, 2, 4, 1, 3):
            cc, device = c_peer(d)
            send(ag_in.at[f, gc, 0:MSG, :], ag_in.at[f, gc, 0:MSG, :], ag_s.at[f, d - 1], ag_r.at[f, gc], device)
        energies.append(jnp.sum(first * first + second * second, axis=0, keepdims=True))

    en1[gr] = jnp.concatenate(energies + [jnp.zeros((8 - NF, 128), F32)], axis=0)
    for d in range(1, 16):
        send(en1.at[gr], en1.at[gr], e1_s.at[d - 1], e1_r.at[gr], g_peer(d)[1])
    for d in range(1, 16):
        gg, device = g_peer(-d)
        arrive(en1.at[gg], e1_s.at[d - 1], e1_r.at[gg], device)
    en2[gc] = functools.reduce(lambda a, b: a + b, [en1[g] for g in range(16)])
    for d in range(1, NC):
        send(en2.at[gc], en2.at[gc], e2_s.at[d - 1], e2_r.at[gc], c_peer(d)[1])

    for f in range(NF):
        for d in range(1, NC):
            cc, device = c_peer(-d)
            arrive(ag_in.at[f, cc, 0:MSG, :], ag_s.at[f, d - 1], ag_r.at[f, cc], device)
        for c in range(NC):
            rows = slice(c * CH, (c + 1) * CH)
            a, b = decode(ag_in[f, c, 0:CH, :], ag_in[f, c, CH : CH + 1, :])
            own_half[rows, :] = jnp.where(gc < 4, a, b)
            a0, a1 = split(a)
            b0, b1 = split(b)
            high_part[rows, 0:128] = a0
            high_part[rows, 128:256] = b0
            low_part[rows, 0:128] = a1
            low_part[rows, 128:256] = b1
        s0, s1 = high_part[...], low_part[...]
        k0 = dot(pick_rows[f], s0).astype(BF16)
        k1 = dot(pick_rows[f], s1).astype(BF16)
        gram_ref[f] = dot_t(k0, k0) + (dot_t(k0, k1) + dot_t(k1, k0))
        cross_ref[f] = dot_t(s0, k0) + (dot_t(s0, k1) + dot_t(s1, k0))
        half_t = jnp.transpose(own_half[...])
        quarter = lax.rem(gc, 4)
        own = half_t[0:32]
        for t in range(1, 4):
            own = jnp.where(quarter == t, half_t[32 * t : 32 * t + 32], own)
        own_ref[f] = own

    for d in range(1, NC):
        cc, device = c_peer(-d)
        arrive(en2.at[cc], e2_s.at[d - 1], e2_r.at[cc], device)
    energy_ref[...] = functools.reduce(lambda a, b: a + b, [en2[c] for c in range(NC)])
    for copy in sends + paced:
        copy.wait_send()


def mm3(a, b):
    a0, a1 = split(a)
    b0, b1 = split(b)
    return dot(a0, b0) + (dot(a0, b1) + dot(a1, b0))


def high(a, b):
    return lax.dot_general(
        a, b, (((1,), (0,)), ((), ())), preferred_element_type=F32, precision=lax.Precision.HIGHEST
    )


def solve_kernel(
    gram_ref, cross_ref, own_ref, energy_ref, coupling_ref,
    own_hbm, basis_hbm, coupling_hbm,
    shifted, state, table, basis, sem,
):
    stores = [
        pltpu.make_async_copy(coupling_ref, coupling_hbm, sem.at[0]),
        pltpu.make_async_copy(own_ref, own_hbm, sem.at[1]),
    ]
    for store in stores:
        store.start()
    eye = diagonal(K, K)
    steps = jnp.zeros((1, 1), F32)
    for f in range(NF):
        energy = jnp.sum(energy_ref[f : f + 1, :], axis=1, keepdims=True)
        level = 0.5 * energy / 8192.0 + 1e-05
        gram = gram_ref[f] + jnp.where(eye, level, 0.0)
        bound = jnp.max(jnp.sum(jnp.abs(gram), axis=0, keepdims=True), axis=1, keepdims=True)
        trace = jnp.sum(
            jnp.sum(jnp.where(eye, gram, 0.0), axis=0, keepdims=True), axis=1, keepdims=True
        )
        top = jnp.minimum(bound, trace)
        c = 2.0 / (level + top)
        low = level * c
        gain = low * (2.0 - low)
        s = 2.0 / (1.0 + gain)
        state[f] = jnp.where(eye, 2.0 * s * c, 0.0) - (s * c * c) * gram
        shifted[f] = gram
        low = s * gain
        needed = jnp.zeros((1, 1), F32)
        for step in range(MOST):
            needed = needed + jnp.where(low < 1.0 - NEAR, 1.0, 0.0)
            gain = low * (2.0 - low)
            s = 2.0 / (1.0 + gain)
            table[f, step : step + 1, :] = jnp.broadcast_to(s, (1, K))
            low = s * gain
        steps = jnp.maximum(steps, needed)

    def improve(step, mm):
        for f in range(NF):
            x = state[f]
            s = table[f, pl.ds(step, 1), :]
            y = (jnp.where(eye, 2.0, 0.0) - mm(shifted[f], x)) * s
            state[f] = mm(x, y)

    count = steps[0, 0].astype(I32)

    @pl.loop(0, count)
    def _(step):
        improve(step, mm3)

    improve(count, high)
    for f in range(NF):
        basis[f] = mm3(cross_ref[f], state[f])
        stores.append(pltpu.make_async_copy(basis.at[f], basis_hbm.at[f], sem.at[2 + f]))
        stores[2 + f].start()
    for store in stores:
        store.wait()


def body(front, omega, child_sketch, child_map, picks):
    child = child_sketch.reshape(NF, 32, R)
    any_space = pl.BlockSpec(memory_space=pltpu.HBM)
    vmem = pl.BlockSpec(memory_space=pltpu.VMEM)
    dma = pltpu.SemaphoreType.DMA
    exchanged = pl.pallas_call(
        exchange_kernel,
        out_shape=(
            jax.ShapeDtypeStruct((NF, K, K), F32),
            jax.ShapeDtypeStruct((NF, LB, K), F32),
            jax.ShapeDtypeStruct((NF, 32, LB), F32),
            jax.ShapeDtypeStruct((8, 128), F32),
            jax.ShapeDtypeStruct((NF, K, 2 * K), BF16),
        ),
        in_specs=[any_space] * 5,
        out_specs=(vmem,) * 5,
        scratch_shapes=[
            pltpu.VMEM((NF, LB, 1024), BF16),
            pltpu.VMEM((NF, 1024, R), BF16),
            pltpu.VMEM((NF, 2, NZ, 32, R), BF16),
            pltpu.VMEM((2, NZ, 8, 128), I32),
            pltpu.VMEM((NF, 2, 16), I32),
            pltpu.VMEM((NF, 16, K), I32),
            pltpu.VMEM((NF, LB, R), F32),
            pltpu.VMEM((NF, NC, SLOT, 128), I32),
            pltpu.VMEM((NF, NC, SLOT, 128), I32),
            pltpu.VMEM((NF, NC, SLOT, 128), I32),
            pltpu.VMEM((16, 8, 128), F32),
            pltpu.VMEM((NC, 8, 128), F32),
            pltpu.VMEM((NF, K, LB), BF16),
            pltpu.VMEM((LB, R), BF16),
            pltpu.VMEM((LB, R), BF16),
            pltpu.VMEM((LB, 128), F32),
            dma((11,)),
            dma((NF, 7)), dma((NF, NZ)),
            dma((8,)), dma((9,)),
            dma((NF,)), dma((NF,)),
            dma((NF, 7)), dma((NF, NC)),
            dma((NF, 7)), dma((NF, NC)),
            dma((15,)), dma((16,)),
            dma((7,)), dma((NC,)),
        ],
        compiler_params=pltpu.CompilerParams(
            collective_id=0, has_side_effects=True, vmem_limit_bytes=48 * 2**20
        ),
        name="exchange",
    )(*(pltpu.with_memory_space_constraint(x, pltpu.HBM) for x in (front, omega, child, child_map, picks)))
    own, basis, coupling = pl.pallas_call(
        solve_kernel,
        out_shape=(
            jax.ShapeDtypeStruct((NF, 32, LB), F32),
            jax.ShapeDtypeStruct((NF, LB, K), F32),
            jax.ShapeDtypeStruct((NF, K, 2 * K), BF16),
        ),
        in_specs=[vmem] * 5,
        out_specs=(any_space,) * 3,
        scratch_shapes=[
            pltpu.VMEM((NF, K, K), F32),
            pltpu.VMEM((NF, K, K), F32),
            pltpu.VMEM((NF, 16, K), F32),
            pltpu.VMEM((NF, LB, K), F32),
            dma((5,)),
        ],
        compiler_params=pltpu.CompilerParams(vmem_limit_bytes=48 * 2**20),
        name="solve",
    )(*exchanged)
    return jnp.transpose(own, (0, 2, 1)), basis, coupling


def solution(mesh):
    return jax.shard_map(
        body,
        mesh=mesh,
        in_specs=(
            P("fr", "gr", "gc"),
            P("fr", "gc", None),
            P("fr", None, ("gr", "gc"), None),
            P("fr", None, ("gr", "gc")),
            P("fr", None, None),
        ),
        out_specs=(P("fr", "gr", "gc"), P("fr", "gr", None), P("fr", "gr", "gc")),
        check_vma=False,
    )
```

```python
import functools
import math

import jax
import jax.numpy as jnp
from jax import lax
from jax.experimental import pallas as pl
from jax.experimental.pallas import tpu as pltpu
from jax.sharding import PartitionSpec as P

MESH = pl.DeviceIdType.MESH
F32 = jnp.float32
BF16 = jnp.bfloat16
I32 = jnp.int32
NF = 3
LB = 512
R = 256
K = 128
NC = 8
NZ = 8
CH = LB // NC
MSG = CH + 1
SLOT = CH + 8
STEP = math.log(2.0) / 8.0
TOP = 32760.0
SMALLEST = 2.0**-110
MOST = 14
NEAR = 3e-3
PEERS = ((1, 2), (1, 1), (1, 3), (0, 2), (1, 0), (0, 1), (0, 3))


def dot(a, b):
    return lax.dot_general(a, b, (((1,), (0,)), ((), ())), preferred_element_type=F32)


def dot_t(a, b):
    return lax.dot_general(a, b, (((1,), (1,)), ((), ())), preferred_element_type=F32)


def split(x):
    hi = x.astype(BF16)
    return hi, (x - hi.astype(F32)).astype(BF16)


def diagonal(rows, columns):
    shape = (rows, columns)
    return lax.broadcasted_iota(I32, shape, 0) == lax.broadcasted_iota(I32, shape, 1)


def encode(x):
    top = jnp.maximum(jnp.max(jnp.abs(x), axis=1, keepdims=True), SMALLEST)
    level = jnp.ceil(jnp.log(top) * (1.0 / STEP))
    q = jnp.round(x * (jnp.exp(level * -STEP) * TOP)).astype(I32)
    packed = (q[:, : R // 2] << 16) | (q[:, R // 2 :] & 0xFFFF)
    levels = jnp.sum(jnp.where(diagonal(CH, 128), level, 0.0), axis=0, keepdims=True)
    return packed, levels.astype(I32)


def decode(packed, levels):
    level = jnp.sum(jnp.where(diagonal(CH, 128), levels.astype(F32), 0.0), axis=1, keepdims=True)
    scale = jnp.exp(level * STEP) * (1.0 / TOP)
    first = (packed >> 16).astype(F32) * scale
    second = ((packed << 16) >> 16).astype(F32) * scale
    return first, second


def exchange_kernel(
    front_hbm, omega_hbm, child_hbm, map_hbm, picks_hbm,
    gram_ref, cross_ref, own_ref, energy_ref, coupling_ref,
    front, omega, child_all, maps, map_in, picks_ref, partial, rs_out, rs_in, ag_in, en1, en2, pick_rows, high_part, low_part, own_half,
    load_sem, child_s, child_r, map_s, map_r, core_s, core_r, rs_s, rs_r, ag_s, ag_r, e1_s, e1_r, e2_s, e2_r,
):
    fr = lax.axis_index("fr")
    gr = lax.axis_index("gr")
    gc = lax.axis_index("gc")
    z = gr // 2
    core = gr % 2

    def z_peer(d):
        zz = lax.rem(z + d + NZ, NZ)
        return zz, (fr, zz * 2 + core, gc)

    def c_peer(d):
        up, right = d
        cc = lax.rem(gc // 4 + up, 2) * 4 + lax.rem(gc % 4 + right, 4)
        return cc, (fr, gr, cc)

    def g_peer(d):
        gg = lax.rem(gr + d + 16, 16)
        return gg, (fr, gg, gc)

    partner = (fr, z * 2 + (1 - core), gc)

    loads = []
    own_child = []
    for f in range(NF):
        own_child.append(pltpu.make_async_copy(child_hbm.at[f], child_all.at[f, core, z], load_sem.at[f]))
        own_child[f].start()
    own_map = pltpu.make_async_copy(map_hbm, map_in, load_sem.at[9])
    own_map.start()
    for f in range(NF):
        a = pltpu.make_async_copy(front_hbm.at[f], front.at[f], load_sem.at[3 + f])
        b = pltpu.make_async_copy(omega_hbm.at[f], omega.at[f], load_sem.at[6 + f])
        b.start()
        a.start()
        loads.append((a, b))

    picks_load = pltpu.make_async_copy(picks_hbm, picks_ref, load_sem.at[10])
    picks_load.start()

    barrier = pltpu.get_barrier_semaphore()
    for d in range(1, 16):
        pl.semaphore_signal(barrier, inc=1, device_id=g_peer(d)[1], device_id_type=MESH)
    for d in PEERS:
        pl.semaphore_signal(barrier, inc=1, device_id=c_peer(d)[1], device_id_type=MESH)
    own_map.wait()
    lane = lax.broadcasted_iota(I32, (1, 128), 1)
    tile = []
    for f in range(NF):
        both = jnp.concatenate([map_in[f, 0:1, :], map_in[f, 1:2, :]] * 4, axis=1)
        tile.append(jnp.where(lane // 32 == z % 4, both, 0))
    maps[core, z] = jnp.concatenate(tile + [jnp.zeros((8 - NF, 128), I32)], axis=0)
    pl.semaphore_wait(barrier, 22)

    sends = []

    def send(src, dst, s, r, device):
        copy = pltpu.make_async_remote_copy(
            src_ref=src, dst_ref=dst, send_sem=s, recv_sem=r, device_id=device, device_id_type=MESH
        )
        copy.start()
        sends.append(copy)

    def arrive(dst, s, r, device):
        pltpu.make_async_remote_copy(
            src_ref=dst, dst_ref=dst, send_sem=s, recv_sem=r, device_id=device, device_id_type=MESH
        ).wait_recv()

    for d in (4, 3, 5, 2, 6, 1, 7):
        device = z_peer(d)[1]
        send(maps.at[core, z, 0:NF, :], maps.at[core, z, 0:NF, :], map_s.at[d - 1], map_r.at[z], device)

    def send_rows(f, origin, to, slot):
        ref = child_all.at[f, core, origin]
        send(ref, ref, child_s.at[f, slot], child_r.at[f, origin], z_peer(to)[1])

    def rows_arrive(f, origin, slot):
        arrive(child_all.at[f, core, origin], child_s.at[f, slot], child_r.at[f, origin], z_peer(1)[1])

    direct = (4, 3, -3, 2, -2, 1, -1)
    def send_children(f):
        own_child[f].wait()
        for slot, d in enumerate(direct):
            send_rows(f, z, d, slot)

    send_children(0)
    send_children(1)
    send_children(2)

    for f in range(NF):
        loads[f][0].wait()
        loads[f][1].wait()
        for half in range(2):
            rows = pl.ds(half * LB, LB)
            off = gr != 2 * gc + half
            omega[f, rows, :] = jnp.where(off, omega[f, rows, :], jnp.zeros((), BF16))
        for r in range(4):
            rows = pl.ds(r * 128, 128)
            partial[f, rows, :] = dot(front[f, rows, :], omega[f])

    picks_load.wait()
    for f in range(NF):
        picked = picks_ref[f, pl.ds(gr, 1), :]
        down = jnp.transpose(jnp.broadcast_to(picked, (K, K)))
        lanes = lax.broadcasted_iota(I32, (K, K), 1)
        pick_rows[f] = jnp.concatenate([(down == lanes + 128 * t).astype(BF16) for t in range(4)], axis=1)
        mine = dot(pick_rows[f], front[f]).astype(BF16)
        for half in range(2):
            wanted = picks_ref[f, pl.ds(2 * gc + half, 1), :]
            pick_columns = (lax.broadcasted_iota(I32, (LB, K), 0) == wanted).astype(BF16)
            coupling_ref[f, :, half * K : (half + 1) * K] = dot(
                mine[:, half * LB : (half + 1) * LB], pick_columns
            ).astype(BF16)

    for d in range(1, NZ):
        zz, device = z_peer(-d)
        arrive(maps.at[core, zz, 0:NF, :], map_s.at[d - 1], map_r.at[zz], device)
    send(maps.at[core], maps.at[core], map_s.at[7], map_r.at[8], partner)

    targets = None
    for f in range(NF):
        for d in direct:
            rows_arrive(f, z_peer(d)[0], 0)
        send(child_all.at[f, core], child_all.at[f, core], core_s.at[f], core_r.at[f], partner)

        if targets is None:
            arrive(maps.at[1 - core], map_s.at[7], map_r.at[8], partner)
            targets = []
            for k in range(2):
                for h in range(2):
                    tile = maps[k, 4 * h]
                    for t in range(1, 4):
                        tile = tile + maps[k, 4 * h + t]
                    targets.append(tile - gr * LB)
        arrive(child_all.at[f, 1 - core], core_s.at[f], core_r.at[f], partner)

        for c in range(NC):
            rows = lax.broadcasted_iota(I32, (CH, 128), 0) + c * CH
            total = partial[f, c * CH : (c + 1) * CH, :]
            hits = jnp.concatenate([(rows == tile[f : f + 1, :]).astype(BF16) for tile in targets], axis=1)
            total = total + dot(hits, child_all[f].reshape(2 * NZ * 32, R))
            partial[f, c * CH : (c + 1) * CH, :] = total
            packed, levels = encode(total)
            rs_out[f, c, 0:CH, :] = packed
            rs_out[f, c, CH:MSG, :] = levels
        for slot, d in enumerate(PEERS):
            cc, device = c_peer(d)
            send(rs_out.at[f, cc, 0:MSG, :], rs_in.at[f, gc, 0:MSG, :], rs_s.at[f, slot], rs_r.at[f, gc], device)

    energies = []
    for f in range(NF):
        own = partial[f, pl.ds(gc * CH, CH), :]
        first, second = own[:, :128], own[:, 128:]
        for d in PEERS:
            cc, device = c_peer(d)
            arrive(rs_in.at[f, cc, 0:MSG, :], rs_s.at[f, 0], rs_r.at[f, cc], device)
            a, b = decode(rs_in[f, cc, 0:CH, :], rs_in[f, cc, CH : CH + 1, :])
            first, second = first + a, second + b
        total = jnp.concatenate([first, second], axis=1)
        packed, levels = encode(total)
        ag_in[f, gc, 0:CH, :] = packed
        ag_in[f, gc, CH:MSG, :] = levels
        for slot, d in enumerate(PEERS):
            cc, device = c_peer(d)
            send(ag_in.at[f, gc, 0:MSG, :], ag_in.at[f, gc, 0:MSG, :], ag_s.at[f, slot], ag_r.at[f, gc], device)
        energies.append(jnp.sum(first * first + second * second, axis=0, keepdims=True))

    en1[gr] = jnp.concatenate(energies + [jnp.zeros((8 - NF, 128), F32)], axis=0)
    for d in range(1, 16):
        send(en1.at[gr], en1.at[gr], e1_s.at[d - 1], e1_r.at[gr], g_peer(d)[1])
    for d in range(1, 16):
        gg, device = g_peer(-d)
        arrive(en1.at[gg], e1_s.at[d - 1], e1_r.at[gg], device)
    en2[gc] = functools.reduce(lambda a, b: a + b, [en1[g] for g in range(16)])
    for slot, d in enumerate(PEERS):
        send(en2.at[gc], en2.at[gc], e2_s.at[slot], e2_r.at[gc], c_peer(d)[1])

    for f in range(NF):
        for d in PEERS:
            cc, device = c_peer(d)
            arrive(ag_in.at[f, cc, 0:MSG, :], ag_s.at[f, 0], ag_r.at[f, cc], device)
        for c in range(NC):
            rows = slice(c * CH, (c + 1) * CH)
            a, b = decode(ag_in[f, c, 0:CH, :], ag_in[f, c, CH : CH + 1, :])
            own_half[rows, :] = jnp.where(gc < 4, a, b)
            a0, a1 = split(a)
            b0, b1 = split(b)
            high_part[rows, 0:128] = a0
            high_part[rows, 128:256] = b0
            low_part[rows, 0:128] = a1
            low_part[rows, 128:256] = b1
        s0, s1 = high_part[...], low_part[...]
        k0 = dot(pick_rows[f], s0).astype(BF16)
        k1 = dot(pick_rows[f], s1).astype(BF16)
        parts = jnp.concatenate([k0, k1], axis=0)
        gram = dot_t(k0, parts)
        gram_ref[f] = gram[:, :K] + (gram[:, K:] + dot_t(k1, k0))
        cross = dot_t(s0, parts)
        cross_ref[f] = cross[:, :K] + (cross[:, K:] + dot_t(s1, k0))
        half_t = jnp.transpose(own_half[...])
        quarter = lax.rem(gc, 4)
        own = half_t[0:32]
        for t in range(1, 4):
            own = jnp.where(quarter == t, half_t[32 * t : 32 * t + 32], own)
        own_ref[f] = own

    for d in PEERS:
        cc, device = c_peer(d)
        arrive(en2.at[cc], e2_s.at[0], e2_r.at[cc], device)
    energy_ref[...] = functools.reduce(lambda a, b: a + b, [en2[c] for c in range(NC)])
    for copy in sends:
        copy.wait_send()


def mm3(a, b):
    left = jnp.concatenate(split(a), axis=1)
    right = jnp.concatenate(split(b), axis=1)
    both = dot(left, jnp.concatenate([right, right], axis=0))
    return both[:, :K] + both[:, K:]


def high(a, b):
    return lax.dot_general(
        a, b, (((1,), (0,)), ((), ())), preferred_element_type=F32, precision=lax.Precision.HIGHEST
    )


def solve_kernel(
    gram_ref, cross_ref, own_ref, energy_ref, coupling_ref,
    own_hbm, basis_hbm, coupling_hbm,
    shifted, state, table, basis, sem,
):
    stores = [
        pltpu.make_async_copy(coupling_ref, coupling_hbm, sem.at[0]),
        pltpu.make_async_copy(own_ref, own_hbm, sem.at[1]),
    ]
    for store in stores:
        store.start()
    eye = diagonal(K, K)
    steps = jnp.zeros((1, 1), F32)
    for f in range(NF):
        energy = jnp.sum(energy_ref[f : f + 1, :], axis=1, keepdims=True)
        level = 0.5 * energy / 8192.0 + 1e-05
        gram = gram_ref[f] + jnp.where(eye, level, 0.0)
        bound = jnp.max(jnp.sum(jnp.abs(gram), axis=0, keepdims=True), axis=1, keepdims=True)
        trace = jnp.sum(
            jnp.sum(jnp.where(eye, gram, 0.0), axis=0, keepdims=True), axis=1, keepdims=True
        )
        top = jnp.minimum(bound, trace)
        c = 2.0 / (level + top)
        low = level * c
        gain = low * (2.0 - low)
        s = 2.0 / (1.0 + gain)
        state[f] = jnp.where(eye, 2.0 * s * c, 0.0) - (s * c * c) * gram
        shifted[f] = gram
        low = s * gain
        needed = jnp.zeros((1, 1), F32)
        for step in range(MOST):
            needed = needed + jnp.where(low < 1.0 - NEAR, 1.0, 0.0)
            gain = low * (2.0 - low)
            s = 2.0 / (1.0 + gain)
            table[f, step : step + 1, :] = jnp.broadcast_to(s, (1, K))
            low = s * gain
        steps = jnp.maximum(steps, needed)

    def improve(step, mm):
        for f in range(NF):
            x = state[f]
            s = table[f, pl.ds(step, 1), :]
            y = (jnp.where(eye, 2.0, 0.0) - mm(shifted[f], x)) * s
            state[f] = mm(x, y)

    count = steps[0, 0].astype(I32)

    @pl.loop(0, count)
    def _(step):
        improve(step, mm3)

    improve(count, high)
    for f in range(NF):
        basis[f] = mm3(cross_ref[f], state[f])
        stores.append(pltpu.make_async_copy(basis.at[f], basis_hbm.at[f], sem.at[2 + f]))
        stores[2 + f].start()
    for store in stores:
        store.wait()


def body(front, omega, child_sketch, child_map, picks):
    child = child_sketch.reshape(NF, 32, R)
    any_space = pl.BlockSpec(memory_space=pltpu.HBM)
    vmem = pl.BlockSpec(memory_space=pltpu.VMEM)
    dma = pltpu.SemaphoreType.DMA
    exchanged = pl.pallas_call(
        exchange_kernel,
        out_shape=(
            jax.ShapeDtypeStruct((NF, K, K), F32),
            jax.ShapeDtypeStruct((NF, LB, K), F32),
            jax.ShapeDtypeStruct((NF, 32, LB), F32),
            jax.ShapeDtypeStruct((8, 128), F32),
            jax.ShapeDtypeStruct((NF, K, 2 * K), BF16),
        ),
        in_specs=[any_space] * 5,
        out_specs=(vmem,) * 5,
        scratch_shapes=[
            pltpu.VMEM((NF, LB, 1024), BF16),
            pltpu.VMEM((NF, 1024, R), BF16),
            pltpu.VMEM((NF, 2, NZ, 32, R), BF16),
            pltpu.VMEM((2, NZ, 8, 128), I32),
            pltpu.VMEM((NF, 2, 16), I32),
            pltpu.VMEM((NF, 16, K), I32),
            pltpu.VMEM((NF, LB, R), F32),
            pltpu.VMEM((NF, NC, SLOT, 128), I32),
            pltpu.VMEM((NF, NC, SLOT, 128), I32),
            pltpu.VMEM((NF, NC, SLOT, 128), I32),
            pltpu.VMEM((16, 8, 128), F32),
            pltpu.VMEM((NC, 8, 128), F32),
            pltpu.VMEM((NF, K, LB), BF16),
            pltpu.VMEM((LB, R), BF16),
            pltpu.VMEM((LB, R), BF16),
            pltpu.VMEM((LB, 128), F32),
            dma((11,)),
            dma((NF, 7)), dma((NF, NZ)),
            dma((8,)), dma((9,)),
            dma((NF,)), dma((NF,)),
            dma((NF, 7)), dma((NF, NC)),
            dma((NF, 7)), dma((NF, NC)),
            dma((15,)), dma((16,)),
            dma((7,)), dma((NC,)),
        ],
        compiler_params=pltpu.CompilerParams(
            collective_id=0, has_side_effects=True, vmem_limit_bytes=48 * 2**20
        ),
        name="exchange",
    )(*(pltpu.with_memory_space_constraint(x, pltpu.HBM) for x in (front, omega, child, child_map, picks)))
    own, basis, coupling = pl.pallas_call(
        solve_kernel,
        out_shape=(
            jax.ShapeDtypeStruct((NF, 32, LB), F32),
            jax.ShapeDtypeStruct((NF, LB, K), F32),
            jax.ShapeDtypeStruct((NF, K, 2 * K), BF16),
        ),
        in_specs=[vmem] * 5,
        out_specs=(any_space,) * 3,
        scratch_shapes=[
            pltpu.VMEM((NF, K, K), F32),
            pltpu.VMEM((NF, K, K), F32),
            pltpu.VMEM((NF, 16, K), F32),
            pltpu.VMEM((NF, LB, K), F32),
            dma((5,)),
        ],
        compiler_params=pltpu.CompilerParams(vmem_limit_bytes=48 * 2**20),
        name="solve",
    )(*exchanged)
    return jnp.transpose(own, (0, 2, 1)), basis, coupling


def solution(mesh):
    return jax.shard_map(
        body,
        mesh=mesh,
        in_specs=(
            P("fr", "gr", "gc"),
            P("fr", "gc", None),
            P("fr", None, ("gr", "gc"), None),
            P("fr", None, ("gr", "gc")),
            P("fr", None, None),
        ),
        out_specs=(P("fr", "gr", "gc"), P("fr", "gr", None), P("fr", "gr", "gc")),
        check_vma=False,
    )
```

```python
import functools
import math

import jax
import jax.numpy as jnp
from jax import lax
from jax.experimental import pallas as pl
from jax.experimental.pallas import tpu as pltpu
from jax.sharding import PartitionSpec as P

MESH = pl.DeviceIdType.MESH
F32 = jnp.float32
BF16 = jnp.bfloat16
I32 = jnp.int32
NF = 3
LB = 512
R = 256
K = 128
NC = 8
NZ = 8
CH = LB // NC
MSG = CH + 1
SLOT = CH + 8
STEP = math.log(2.0) / 8.0
TOP = 32760.0
SMALLEST = 2.0**-110
NEAR = 3e-3
OTHER_CORE = (4, -3, 3, -2, 2, -1, 1)
PEERS = ((1, 2), (1, 1), (1, 3), (1, 0), (0, 2), (0, 1), (0, 3))


def thresholds(count):
    low, table = 1.0 - NEAR, []
    for _ in range(count):
        table.append(low)
        gain = low / (2.0 - low)
        low = gain / (1.0 + math.sqrt(1.0 - gain))
    return table


def dot(a, b):
    return lax.dot_general(a, b, (((1,), (0,)), ((), ())), preferred_element_type=F32)


def dot_t(a, b):
    return lax.dot_general(a, b, (((1,), (1,)), ((), ())), preferred_element_type=F32)


def split(x):
    hi = x.astype(BF16)
    return hi, (x - hi.astype(F32)).astype(BF16)


def diagonal(rows, columns):
    shape = (rows, columns)
    return lax.broadcasted_iota(I32, shape, 0) == lax.broadcasted_iota(I32, shape, 1)


def encode(x):
    top = jnp.maximum(jnp.max(jnp.abs(x), axis=1, keepdims=True), SMALLEST)
    level = jnp.ceil(jnp.log(top) * (1.0 / STEP))
    q = jnp.round(x * (jnp.exp(level * -STEP) * TOP)).astype(I32)
    packed = (q[:, : R // 2] << 16) | (q[:, R // 2 :] & 0xFFFF)
    levels = jnp.sum(jnp.where(diagonal(CH, 128), level, 0.0), axis=0, keepdims=True)
    return packed, levels.astype(I32)


def decode(packed, levels):
    level = jnp.sum(jnp.where(diagonal(CH, 128), levels.astype(F32), 0.0), axis=1, keepdims=True)
    scale = jnp.exp(level * STEP) * (1.0 / TOP)
    first = (packed >> 16).astype(F32) * scale
    second = ((packed << 16) >> 16).astype(F32) * scale
    return first, second


def exchange_kernel(
    front_hbm, omega_hbm, child_hbm, map_hbm, picks_hbm,
    gram_ref, cross_ref, own_ref, energy_ref, coupling_ref,
    front, omega, child_all, maps, map_in, picks_ref, partial, rs_out, rs_in, ag_in, en1, en2, pick_rows, high_part, low_part, own_half,
    load_sem, child_s, child_r, map_s, map_r, core_s, core_r, rs_s, rs_r, ag_s, ag_r, e1_s, e1_r, e2_s, e2_r,
):
    fr = lax.axis_index("fr")
    gr = lax.axis_index("gr")
    gc = lax.axis_index("gc")
    z = gr // 2
    core = gr % 2

    def z_peer(d):
        zz = lax.rem(z + d + NZ, NZ)
        return zz, (fr, zz * 2 + core, gc)

    def c_peer(d):
        up, right = d
        cc = lax.rem(gc // 4 + up, 2) * 4 + lax.rem(gc % 4 + right + core * 2 * (right % 2), 4)
        return cc, (fr, gr, cc)

    def g_peer(d):
        gg = lax.rem(gr + d + 16, 16)
        return gg, (fr, gg, gc)

    partner = (fr, z * 2 + (1 - core), gc)

    loads = []
    own_child = []
    for f in range(NF):
        own_child.append(pltpu.make_async_copy(child_hbm.at[f], child_all.at[f, core, z], load_sem.at[f]))
        own_child[f].start()
    own_map = pltpu.make_async_copy(map_hbm, map_in, load_sem.at[9])
    own_map.start()
    for f in range(NF):
        a = pltpu.make_async_copy(front_hbm.at[f], front.at[f], load_sem.at[3 + f])
        b = pltpu.make_async_copy(omega_hbm.at[f], omega.at[f], load_sem.at[6 + f])
        b.start()
        a.start()
        loads.append((a, b))

    picks_load = pltpu.make_async_copy(picks_hbm, picks_ref, load_sem.at[10])
    picks_load.start()

    barrier = pltpu.get_barrier_semaphore()
    for d in range(1, 16):
        pl.semaphore_signal(barrier, inc=1, device_id=g_peer(d)[1], device_id_type=MESH)
    for d in PEERS:
        pl.semaphore_signal(barrier, inc=1, device_id=c_peer(d)[1], device_id_type=MESH)
    own_map.wait()
    lane = lax.broadcasted_iota(I32, (1, 128), 1)
    tile = []
    for f in range(NF):
        both = jnp.concatenate([map_in[f, 0:1, :], map_in[f, 1:2, :]] * 4, axis=1)
        tile.append(jnp.where(lane // 32 == z % 4, both, 0))
    maps[core, z] = jnp.concatenate(tile + [jnp.zeros((8 - NF, 128), I32)], axis=0)
    pl.semaphore_wait(barrier, 22)

    sends = []

    def send(src, dst, s, r, device):
        copy = pltpu.make_async_remote_copy(
            src_ref=src, dst_ref=dst, send_sem=s, recv_sem=r, device_id=device, device_id_type=MESH
        )
        copy.start()
        sends.append(copy)

    def arrive(dst, s, r, device):
        pltpu.make_async_remote_copy(
            src_ref=dst, dst_ref=dst, send_sem=s, recv_sem=r, device_id=device, device_id_type=MESH
        ).wait_recv()

    for d in (4, 3, 5, 2, 6, 1, 7):
        device = z_peer(d)[1]
        send(maps.at[core, z, 0:NF, :], maps.at[core, z, 0:NF, :], map_s.at[d - 1], map_r.at[z], device)

    def send_rows(f, origin, to, slot):
        ref = child_all.at[f, core, origin]
        send(ref, ref, child_s.at[f, slot], child_r.at[f, origin], z_peer(to)[1])

    def rows_arrive(f, origin, slot):
        arrive(child_all.at[f, core, origin], child_s.at[f, slot], child_r.at[f, origin], z_peer(1)[1])

    direct = (4, 3, -3, 2, -2, 1, -1)
    def send_children(f):
        own_child[f].wait()
        for slot, pair in enumerate(zip(direct, OTHER_CORE)):
            send_rows(f, z, jnp.where(core == 0, *pair), slot)

    send_children(0)
    send_children(1)
    send_children(2)

    for f in range(NF):
        loads[f][0].wait()
        loads[f][1].wait()
        for half in range(2):
            rows = pl.ds(half * LB, LB)
            off = gr != 2 * gc + half
            omega[f, rows, :] = jnp.where(off, omega[f, rows, :], jnp.zeros((), BF16))
        for r in range(4):
            rows = pl.ds(r * 128, 128)
            partial[f, rows, :] = dot(front[f, rows, :], omega[f])

    picks_load.wait()
    for f in range(NF):
        picked = picks_ref[f, pl.ds(gr, 1), :]
        down = jnp.transpose(jnp.broadcast_to(picked, (K, K)))
        lanes = lax.broadcasted_iota(I32, (K, K), 1)
        pick_rows[f] = jnp.concatenate([(down == lanes + 128 * t).astype(BF16) for t in range(4)], axis=1)
        mine = dot(pick_rows[f], front[f]).astype(BF16)
        for half in range(2):
            wanted = picks_ref[f, pl.ds(2 * gc + half, 1), :]
            pick_columns = (lax.broadcasted_iota(I32, (LB, K), 0) == wanted).astype(BF16)
            coupling_ref[f, :, half * K : (half + 1) * K] = dot(
                mine[:, half * LB : (half + 1) * LB], pick_columns
            ).astype(BF16)

    for d in range(1, NZ):
        zz, device = z_peer(-d)
        arrive(maps.at[core, zz, 0:NF, :], map_s.at[d - 1], map_r.at[zz], device)
    send(maps.at[core], maps.at[core], map_s.at[7], map_r.at[8], partner)

    targets = None
    for f in range(NF):
        for d in direct:
            rows_arrive(f, z_peer(d)[0], 0)
        send(child_all.at[f, core], child_all.at[f, core], core_s.at[f], core_r.at[f], partner)

        if targets is None:
            arrive(maps.at[1 - core], map_s.at[7], map_r.at[8], partner)
            targets = []
            for k in range(2):
                for h in range(2):
                    tile = maps[k, 4 * h]
                    for t in range(1, 4):
                        tile = tile + maps[k, 4 * h + t]
                    targets.append(tile - gr * LB)
        arrive(child_all.at[f, 1 - core], core_s.at[f], core_r.at[f], partner)

        rows = lax.broadcasted_iota(I32, (LB, 128), 0)
        hits = jnp.concatenate([(rows == tile[f : f + 1, :]).astype(BF16) for tile in targets], axis=1)
        whole = partial[f] + dot(hits, child_all[f].reshape(2 * NZ * 32, R))
        partial[f] = whole
        for c in range(NC):
            packed, levels = encode(whole[c * CH : (c + 1) * CH])
            rs_out[f, c, 0:CH, :] = packed
            rs_out[f, c, CH:MSG, :] = levels
        for slot, d in enumerate(PEERS):
            cc, device = c_peer(d)
            send(rs_out.at[f, cc, 0:MSG, :], rs_in.at[f, gc, 0:MSG, :], rs_s.at[f, slot], rs_r.at[f, gc], device)

    energies = []
    for f in range(NF):
        own = partial[f, pl.ds(gc * CH, CH), :]
        first, second = own[:, :128], own[:, 128:]
        for d in PEERS:
            cc, device = c_peer(d)
            arrive(rs_in.at[f, cc, 0:MSG, :], rs_s.at[f, 0], rs_r.at[f, cc], device)
        for d in PEERS:
            cc = c_peer(d)[0]
            a, b = decode(rs_in[f, cc, 0:CH, :], rs_in[f, cc, CH : CH + 1, :])
            first, second = first + a, second + b
        total = jnp.concatenate([first, second], axis=1)
        packed, levels = encode(total)
        ag_in[f, gc, 0:CH, :] = packed
        ag_in[f, gc, CH:MSG, :] = levels
        energies.append(jnp.sum(first * first + second * second, axis=0, keepdims=True))
        if f == NF - 1:
            en1[gr] = jnp.concatenate(energies + [jnp.zeros((8 - NF, 128), F32)], axis=0)
            for d in range(1, 16):
                send(en1.at[gr], en1.at[gr], e1_s.at[d - 1], e1_r.at[gr], g_peer(d)[1])
        for slot, d in enumerate(PEERS):
            cc, device = c_peer(d)
            send(ag_in.at[f, gc, 0:MSG, :], ag_in.at[f, gc, 0:MSG, :], ag_s.at[f, slot], ag_r.at[f, gc], device)

    for d in range(1, 16):
        gg, device = g_peer(-d)
        arrive(en1.at[gg], e1_s.at[d - 1], e1_r.at[gg], device)
    en2[gc] = functools.reduce(lambda a, b: a + b, [en1[g] for g in range(16)])
    for slot, d in enumerate(PEERS):
        send(en2.at[gc], en2.at[gc], e2_s.at[slot], e2_r.at[gc], c_peer(d)[1])

    for f in range(NF):
        if f == NF - 1:
            for copy in sends:
                copy.wait_send()
        for d in PEERS:
            cc, device = c_peer(d)
            arrive(ag_in.at[f, cc, 0:MSG, :], ag_s.at[f, 0], ag_r.at[f, cc], device)
        for c in range(NC):
            rows = slice(c * CH, (c + 1) * CH)
            a, b = decode(ag_in[f, c, 0:CH, :], ag_in[f, c, CH : CH + 1, :])
            own_half[rows, :] = jnp.where(gc < 4, a, b)
            a0, a1 = split(a)
            b0, b1 = split(b)
            high_part[rows, 0:128] = a0
            high_part[rows, 128:256] = b0
            low_part[rows, 0:128] = a1
            low_part[rows, 128:256] = b1
        s0, s1 = high_part[...], low_part[...]
        k0 = dot(pick_rows[f], s0).astype(BF16)
        k1 = dot(pick_rows[f], s1).astype(BF16)
        parts = jnp.concatenate([k0, k1], axis=0)
        gram = dot_t(k0, parts)
        gram_ref[f] = gram[:, :K] + (gram[:, K:] + dot_t(k1, k0))
        cross = dot_t(s0, parts)
        cross_ref[f] = cross[:, :K] + (cross[:, K:] + dot_t(s1, k0))
        half_t = jnp.transpose(own_half[...])
        quarter = lax.rem(gc, 4)
        own = half_t[0:32]
        for t in range(1, 4):
            own = jnp.where(quarter == t, half_t[32 * t : 32 * t + 32], own)
        own_ref[f] = own

    for d in PEERS:
        cc, device = c_peer(d)
        arrive(en2.at[cc], e2_s.at[0], e2_r.at[cc], device)
    energy_ref[...] = functools.reduce(lambda a, b: a + b, [en2[c] for c in range(NC)])


def mm3(a, b):
    left = jnp.concatenate(split(a), axis=1)
    right = jnp.concatenate(split(b), axis=1)
    both = dot(left, jnp.concatenate([right, right], axis=0))
    return both[:, :K] + both[:, K:]


def high(a, b):
    return lax.dot_general(
        a, b, (((1,), (0,)), ((), ())), preferred_element_type=F32, precision=lax.Precision.HIGHEST
    )


def solve_kernel(
    gram_ref, cross_ref, own_ref, energy_ref, coupling_ref,
    own_hbm, basis_hbm, coupling_hbm,
    shifted, state, lows, basis, sem,
):
    stores = [
        pltpu.make_async_copy(coupling_ref, coupling_hbm, sem.at[0]),
        pltpu.make_async_copy(own_ref, own_hbm, sem.at[1]),
    ]
    for store in stores:
        store.start()
    eye = diagonal(K, K)
    steps = jnp.zeros((1, 1), F32)
    for f in range(NF):
        energy = jnp.sum(energy_ref[f : f + 1, :], axis=1, keepdims=True)
        level = 0.5 * energy / 8192.0 + 1e-05
        gram = gram_ref[f] + jnp.where(eye, level, 0.0)
        bound = jnp.max(jnp.sum(jnp.abs(gram), axis=0, keepdims=True), axis=1, keepdims=True)
        trace = jnp.sum(
            jnp.sum(jnp.where(eye, gram, 0.0), axis=0, keepdims=True), axis=1, keepdims=True
        )
        top = jnp.minimum(bound, trace)
        c = 2.0 / (level + top)
        low = level * c
        gain = low * (2.0 - low)
        s = 2.0 / (1.0 + gain)
        state[f] = jnp.where(eye, 2.0 * s * c, 0.0) - (s * c * c) * gram
        shifted[f] = gram
        low = s * gain
        lows[f : f + 1, :] = jnp.broadcast_to(low, (1, K))
        needed = jnp.zeros((1, 1), F32)
        for mark in thresholds(14):
            needed = needed + jnp.where(low < mark, 1.0, 0.0)
        steps = jnp.maximum(steps, needed)

    def improve(mm):
        for f in range(NF):
            x = state[f]
            low = lows[f : f + 1, :]
            gain = low * (2.0 - low)
            s = 2.0 / (1.0 + gain)
            lows[f : f + 1, :] = s * gain
            y = (jnp.where(eye, 2.0, 0.0) - mm(shifted[f], x)) * s
            state[f] = mm(x, y)

    count = steps[0, 0].astype(I32)

    @pl.loop(0, count)
    def _(step):
        improve(mm3)

    improve(high)
    for f in range(NF):
        basis[f] = mm3(cross_ref[f], state[f])
        stores.append(pltpu.make_async_copy(basis.at[f], basis_hbm.at[f], sem.at[2 + f]))
        stores[2 + f].start()
    for store in stores:
        store.wait()


def body(front, omega, child_sketch, child_map, picks):
    child = child_sketch.reshape(NF, 32, R)
    any_space = pl.BlockSpec(memory_space=pltpu.HBM)
    vmem = pl.BlockSpec(memory_space=pltpu.VMEM)
    dma = pltpu.SemaphoreType.DMA
    exchanged = pl.pallas_call(
        exchange_kernel,
        out_shape=(
            jax.ShapeDtypeStruct((NF, K, K), F32),
            jax.ShapeDtypeStruct((NF, LB, K), F32),
            jax.ShapeDtypeStruct((NF, 32, LB), F32),
            jax.ShapeDtypeStruct((8, 128), F32),
            jax.ShapeDtypeStruct((NF, K, 2 * K), BF16),
        ),
        in_specs=[any_space] * 5,
        out_specs=(vmem,) * 5,
        scratch_shapes=[
            pltpu.VMEM((NF, LB, 1024), BF16),
            pltpu.VMEM((NF, 1024, R), BF16),
            pltpu.VMEM((NF, 2, NZ, 32, R), BF16),
            pltpu.VMEM((2, NZ, 8, 128), I32),
            pltpu.VMEM((NF, 2, 16), I32),
            pltpu.VMEM((NF, 16, K), I32),
            pltpu.VMEM((NF, LB, R), F32),
            pltpu.VMEM((NF, NC, SLOT, 128), I32),
            pltpu.VMEM((NF, NC, SLOT, 128), I32),
            pltpu.VMEM((NF, NC, SLOT, 128), I32),
            pltpu.VMEM((16, 8, 128), F32),
            pltpu.VMEM((NC, 8, 128), F32),
            pltpu.VMEM((NF, K, LB), BF16),
            pltpu.VMEM((LB, R), BF16),
            pltpu.VMEM((LB, R), BF16),
            pltpu.VMEM((LB, 128), F32),
            dma((11,)),
            dma((NF, 7)), dma((NF, NZ)),
            dma((8,)), dma((9,)),
            dma((NF,)), dma((NF,)),
            dma((NF, 7)), dma((NF, NC)),
            dma((NF, 7)), dma((NF, NC)),
            dma((15,)), dma((16,)),
            dma((7,)), dma((NC,)),
        ],
        compiler_params=pltpu.CompilerParams(
            collective_id=0, has_side_effects=True, vmem_limit_bytes=48 * 2**20
        ),
        name="exchange",
    )(*(pltpu.with_memory_space_constraint(x, pltpu.HBM) for x in (front, omega, child, child_map, picks)))
    own, basis, coupling = pl.pallas_call(
        solve_kernel,
        out_shape=(
            jax.ShapeDtypeStruct((NF, 32, LB), F32),
            jax.ShapeDtypeStruct((NF, LB, K), F32),
            jax.ShapeDtypeStruct((NF, K, 2 * K), BF16),
        ),
        in_specs=[vmem] * 5,
        out_specs=(any_space,) * 3,
        scratch_shapes=[
            pltpu.VMEM((NF, K, K), F32),
            pltpu.VMEM((NF, K, K), F32),
            pltpu.VMEM((8, K), F32),
            pltpu.VMEM((NF, LB, K), F32),
            dma((5,)),
        ],
        compiler_params=pltpu.CompilerParams(vmem_limit_bytes=48 * 2**20),
        name="solve",
    )(*exchanged)
    return jnp.transpose(own, (0, 2, 1)), basis, coupling


def solution(mesh):
    return jax.shard_map(
        body,
        mesh=mesh,
        in_specs=(
            P("fr", "gr", "gc"),
            P("fr", "gc", None),
            P("fr", None, ("gr", "gc"), None),
            P("fr", None, ("gr", "gc")),
            P("fr", None, None),
        ),
        out_specs=(P("fr", "gr", "gc"), P("fr", "gr", None), P("fr", "gr", "gc")),
        check_vma=False,
    )
```

```python
import functools
import math

import jax
import jax.numpy as jnp
from jax import lax
from jax.experimental import pallas as pl
from jax.experimental.pallas import tpu as pltpu
from jax.sharding import PartitionSpec as P

MESH = pl.DeviceIdType.MESH
F32 = jnp.float32
BF16 = jnp.bfloat16
I32 = jnp.int32
NF = 3
LB = 512
R = 256
K = 128
NC = 8
NZ = 8
CH = LB // NC
MSG = CH + 1
SLOT = CH + 8
STEP = math.log(2.0) / 8.0
TOP = 32760.0
SMALLEST = 2.0**-110
NEAR = 3e-3
OTHER_CORE = (4, -3, 3, -2, 2, -1, 1)
PEERS = ((1, 2), (1, 1), (1, 3), (1, 0), (0, 2), (0, 1), (0, 3))


def thresholds(count):
    low, table = 1.0 - NEAR, []
    for _ in range(count):
        table.append(low)
        gain = low / (2.0 - low)
        low = gain / (1.0 + math.sqrt(1.0 - gain))
    return table


def dot(a, b):
    return lax.dot_general(a, b, (((1,), (0,)), ((), ())), preferred_element_type=F32)


def dot_t(a, b):
    return lax.dot_general(a, b, (((1,), (1,)), ((), ())), preferred_element_type=F32)


def split(x):
    hi = x.astype(BF16)
    return hi, (x - hi.astype(F32)).astype(BF16)


def diagonal(rows, columns):
    shape = (rows, columns)
    return lax.broadcasted_iota(I32, shape, 0) == lax.broadcasted_iota(I32, shape, 1)


def encode(x):
    top = jnp.maximum(jnp.max(jnp.abs(x), axis=1, keepdims=True), SMALLEST)
    level = jnp.ceil(jnp.log(top) * (1.0 / STEP))
    q = jnp.round(x * (jnp.exp(level * -STEP) * TOP)).astype(I32)
    packed = (q[:, : R // 2] << 16) | (q[:, R // 2 :] & 0xFFFF)
    levels = jnp.sum(jnp.where(diagonal(CH, 128), level, 0.0), axis=0, keepdims=True)
    return packed, levels.astype(I32)


def decode(packed, levels):
    level = jnp.sum(jnp.where(diagonal(CH, 128), levels.astype(F32), 0.0), axis=1, keepdims=True)
    scale = jnp.exp(level * STEP) * (1.0 / TOP)
    first = (packed >> 16).astype(F32) * scale
    second = ((packed << 16) >> 16).astype(F32) * scale
    return first, second


def exchange_kernel(
    front_hbm, omega_hbm, child_hbm, map_hbm, picks_hbm,
    gram_ref, cross_ref, own_ref, energy_ref, coupling_ref,
    front, omega, child_all, maps, map_in, picks_ref, partial, rs_out, rs_in, ag_in, en1, en2, pick_rows, high_part, low_part, own_half,
    load_sem, child_s, child_r, map_s, map_r, core_s, core_r, rs_s, rs_r, ag_s, ag_r, e1_s, e1_r, e2_s, e2_r,
):
    fr = lax.axis_index("fr")
    gr = lax.axis_index("gr")
    gc = lax.axis_index("gc")
    z = gr // 2
    core = gr % 2

    def z_peer(d):
        zz = lax.rem(z + d + NZ, NZ)
        return zz, (fr, zz * 2 + core, gc)

    def c_peer(d):
        up, right = d
        cc = lax.rem(gc // 4 + up, 2) * 4 + lax.rem(gc % 4 + right + core * 2 * (right % 2), 4)
        return cc, (fr, gr, cc)

    def g_peer(d):
        gg = lax.rem(gr + d + 16, 16)
        return gg, (fr, gg, gc)

    partner = (fr, z * 2 + (1 - core), gc)

    barrier = pltpu.get_barrier_semaphore()
    for d in range(1, 16):
        pl.semaphore_signal(barrier, inc=1, device_id=g_peer(d)[1], device_id_type=MESH)
    for d in PEERS:
        pl.semaphore_signal(barrier, inc=1, device_id=c_peer(d)[1], device_id_type=MESH)

    loads = []
    own_child = []
    for f in range(NF):
        own_child.append(pltpu.make_async_copy(child_hbm.at[f], child_all.at[f, core, z], load_sem.at[f]))
        own_child[f].start()
    own_map = pltpu.make_async_copy(map_hbm, map_in, load_sem.at[9])
    own_map.start()
    for f in range(NF):
        a = pltpu.make_async_copy(front_hbm.at[f], front.at[f], load_sem.at[3 + f])
        b = pltpu.make_async_copy(omega_hbm.at[f], omega.at[f], load_sem.at[6 + f])
        b.start()
        a.start()
        loads.append((a, b))

    picks_load = pltpu.make_async_copy(picks_hbm, picks_ref, load_sem.at[10])
    picks_load.start()

    own_map.wait()
    lane = lax.broadcasted_iota(I32, (1, 128), 1)
    tile = []
    for f in range(NF):
        both = jnp.concatenate([map_in[f, 0:1, :], map_in[f, 1:2, :]] * 4, axis=1)
        tile.append(jnp.where(lane // 32 == z % 4, both, 0))
    maps[core, z] = jnp.concatenate(tile + [jnp.zeros((8 - NF, 128), I32)], axis=0)
    pl.semaphore_wait(barrier, 22)

    sends = []

    def send(src, dst, s, r, device):
        copy = pltpu.make_async_remote_copy(
            src_ref=src, dst_ref=dst, send_sem=s, recv_sem=r, device_id=device, device_id_type=MESH
        )
        copy.start()
        sends.append(copy)

    def arrive(dst, s, r, device):
        pltpu.make_async_remote_copy(
            src_ref=dst, dst_ref=dst, send_sem=s, recv_sem=r, device_id=device, device_id_type=MESH
        ).wait_recv()

    for d in (4, 3, 5, 2, 6, 1, 7):
        device = z_peer(d)[1]
        send(maps.at[core, z, 0:NF, :], maps.at[core, z, 0:NF, :], map_s.at[d - 1], map_r.at[z], device)

    def send_rows(f, origin, to, slot):
        ref = child_all.at[f, core, origin]
        send(ref, ref, child_s.at[f, slot], child_r.at[f, origin], z_peer(to)[1])

    def rows_arrive(f, origin, slot):
        arrive(child_all.at[f, core, origin], child_s.at[f, slot], child_r.at[f, origin], z_peer(1)[1])

    direct = (4, 3, -3, 2, -2, 1, -1)
    def send_children(f):
        own_child[f].wait()
        for slot, pair in enumerate(zip(direct, OTHER_CORE)):
            send_rows(f, z, jnp.where(core == 0, *pair), slot)

    send_children(0)
    send_children(1)
    send_children(2)

    for f in range(NF):
        loads[f][0].wait()
        loads[f][1].wait()
        for half in range(2):
            rows = pl.ds(half * LB, LB)
            off = gr != 2 * gc + half
            omega[f, rows, :] = jnp.where(off, omega[f, rows, :], jnp.zeros((), BF16))
        for r in range(4):
            rows = pl.ds(r * 128, 128)
            partial[f, rows, :] = dot(front[f, rows, :], omega[f])

    picks_load.wait()
    for f in range(NF):
        picked = picks_ref[f, pl.ds(gr, 1), :]
        down = jnp.transpose(jnp.broadcast_to(picked, (K, K)))
        lanes = lax.broadcasted_iota(I32, (K, K), 1)
        pick_rows[f] = jnp.concatenate([(down == lanes + 128 * t).astype(BF16) for t in range(4)], axis=1)
        mine = dot(pick_rows[f], front[f]).astype(BF16)
        for half in range(2):
            wanted = picks_ref[f, pl.ds(2 * gc + half, 1), :]
            pick_columns = (lax.broadcasted_iota(I32, (LB, K), 0) == wanted).astype(BF16)
            coupling_ref[f, :, half * K : (half + 1) * K] = dot(
                mine[:, half * LB : (half + 1) * LB], pick_columns
            ).astype(BF16)

    for d in range(1, NZ):
        zz, device = z_peer(-d)
        arrive(maps.at[core, zz, 0:NF, :], map_s.at[d - 1], map_r.at[zz], device)
    send(maps.at[core], maps.at[core], map_s.at[7], map_r.at[8], partner)

    targets = None
    for f in range(NF):
        for d in direct:
            rows_arrive(f, z_peer(d)[0], 0)
        send(child_all.at[f, core], child_all.at[f, core], core_s.at[f], core_r.at[f], partner)

        if targets is None:
            arrive(maps.at[1 - core], map_s.at[7], map_r.at[8], partner)
            targets = []
            for k in range(2):
                for h in range(2):
                    tile = maps[k, 4 * h]
                    for t in range(1, 4):
                        tile = tile + maps[k, 4 * h + t]
                    targets.append(tile - gr * LB)
        arrive(child_all.at[f, 1 - core], core_s.at[f], core_r.at[f], partner)

        rows = lax.broadcasted_iota(I32, (LB, 128), 0)
        hits = jnp.concatenate([(rows == tile[f : f + 1, :]).astype(BF16) for tile in targets], axis=1)
        whole = partial[f] + dot(hits, child_all[f].reshape(2 * NZ * 32, R))
        partial[f] = whole
        for c in range(NC):
            packed, levels = encode(whole[c * CH : (c + 1) * CH])
            rs_out[f, c, 0:CH, :] = packed
            rs_out[f, c, CH:MSG, :] = levels
        for slot, d in enumerate(PEERS):
            cc, device = c_peer(d)
            send(rs_out.at[f, cc, 0:MSG, :], rs_in.at[f, gc, 0:MSG, :], rs_s.at[f, slot], rs_r.at[f, gc], device)

    energies = []
    for f in range(NF):
        own = partial[f, pl.ds(gc * CH, CH), :]
        first, second = own[:, :128], own[:, 128:]
        for d in PEERS:
            cc, device = c_peer(d)
            arrive(rs_in.at[f, cc, 0:MSG, :], rs_s.at[f, 0], rs_r.at[f, cc], device)
        for d in PEERS:
            cc = c_peer(d)[0]
            a, b = decode(rs_in[f, cc, 0:CH, :], rs_in[f, cc, CH : CH + 1, :])
            first, second = first + a, second + b
        total = jnp.concatenate([first, second], axis=1)
        packed, levels = encode(total)
        ag_in[f, gc, 0:CH, :] = packed
        ag_in[f, gc, CH:MSG, :] = levels
        energies.append(jnp.sum(first * first + second * second, axis=0, keepdims=True))
        if f == NF - 1:
            en1[gr] = jnp.concatenate(energies + [jnp.zeros((8 - NF, 128), F32)], axis=0)
            for d in range(1, 16):
                send(en1.at[gr, 0:NF, :], en1.at[gr, 0:NF, :], e1_s.at[d - 1], e1_r.at[gr], g_peer(d)[1])
        for slot, d in enumerate(PEERS):
            cc, device = c_peer(d)
            send(ag_in.at[f, gc, 0:MSG, :], ag_in.at[f, gc, 0:MSG, :], ag_s.at[f, slot], ag_r.at[f, gc], device)

    for d in range(1, 16):
        gg, device = g_peer(-d)
        arrive(en1.at[gg, 0:NF, :], e1_s.at[d - 1], e1_r.at[gg], device)
    en2[gc] = functools.reduce(lambda a, b: a + b, [en1[g] for g in range(16)])
    for slot, d in enumerate(PEERS):
        send(en2.at[gc, 0:NF, :], en2.at[gc, 0:NF, :], e2_s.at[slot], e2_r.at[gc], c_peer(d)[1])

    for f in range(NF):
        if f == NF - 1:
            for copy in sends:
                copy.wait_send()
        for d in PEERS:
            cc, device = c_peer(d)
            arrive(ag_in.at[f, cc, 0:MSG, :], ag_s.at[f, 0], ag_r.at[f, cc], device)
        for c in range(NC):
            rows = slice(c * CH, (c + 1) * CH)
            a, b = decode(ag_in[f, c, 0:CH, :], ag_in[f, c, CH : CH + 1, :])
            own_half[rows, :] = jnp.where(gc < 4, a, b)
            a0, a1 = split(a)
            b0, b1 = split(b)
            high_part[rows, 0:128] = a0
            high_part[rows, 128:256] = b0
            low_part[rows, 0:128] = a1
            low_part[rows, 128:256] = b1
        s0, s1 = high_part[...], low_part[...]
        k0 = dot(pick_rows[f], s0).astype(BF16)
        k1 = dot(pick_rows[f], s1).astype(BF16)
        parts = jnp.concatenate([k0, k1], axis=0)
        gram = dot_t(k0, parts)
        gram_ref[f] = gram[:, :K] + (gram[:, K:] + dot_t(k1, k0))
        cross = dot_t(s0, parts)
        cross_ref[f] = cross[:, :K] + (cross[:, K:] + dot_t(s1, k0))
        half_t = jnp.transpose(own_half[...])
        quarter = lax.rem(gc, 4)
        own = half_t[0:32]
        for t in range(1, 4):
            own = jnp.where(quarter == t, half_t[32 * t : 32 * t + 32], own)
        own_ref[f] = own

    for d in PEERS:
        cc, device = c_peer(d)
        arrive(en2.at[cc, 0:NF, :], e2_s.at[0], e2_r.at[cc], device)
    energy_ref[...] = functools.reduce(lambda a, b: a + b, [en2[c] for c in range(NC)])


def mm3(a, b):
    left = jnp.concatenate(split(a), axis=1)
    right = jnp.concatenate(split(b), axis=1)
    both = dot(left, jnp.concatenate([right, right], axis=0))
    return both[:, :K] + both[:, K:]


def high(a, b):
    return lax.dot_general(
        a, b, (((1,), (0,)), ((), ())), preferred_element_type=F32, precision=lax.Precision.HIGHEST
    )


def solve_kernel(
    gram_ref, cross_ref, own_ref, energy_ref, coupling_ref,
    own_hbm, basis_hbm, coupling_hbm,
    shifted, state, lows, basis, sem,
):
    stores = [
        pltpu.make_async_copy(coupling_ref, coupling_hbm, sem.at[0]),
        pltpu.make_async_copy(own_ref, own_hbm, sem.at[1]),
    ]
    for store in stores:
        store.start()
    eye = diagonal(K, K)
    steps = jnp.zeros((1, 1), F32)
    for f in range(NF):
        energy = jnp.sum(energy_ref[f : f + 1, :], axis=1, keepdims=True)
        level = 0.5 * energy / 8192.0 + 1e-05
        gram = gram_ref[f] + jnp.where(eye, level, 0.0)
        bound = jnp.max(jnp.sum(jnp.abs(gram), axis=0, keepdims=True), axis=1, keepdims=True)
        trace = jnp.sum(
            jnp.sum(jnp.where(eye, gram, 0.0), axis=0, keepdims=True), axis=1, keepdims=True
        )
        top = jnp.minimum(bound, trace)
        c = 2.0 / (level + top)
        low = level * c
        gain = low * (2.0 - low)
        s = 2.0 / (1.0 + gain)
        state[f] = jnp.where(eye, 2.0 * s * c, 0.0) - (s * c * c) * gram
        shifted[f] = gram
        low = s * gain
        lows[f : f + 1, :] = jnp.broadcast_to(low, (1, K))
        needed = jnp.zeros((1, 1), F32)
        for mark in thresholds(14):
            needed = needed + jnp.where(low < mark, 1.0, 0.0)
        steps = jnp.maximum(steps, needed)

    def improve(mm):
        for f in range(NF):
            x = state[f]
            low = lows[f : f + 1, :]
            gain = low * (2.0 - low)
            s = 2.0 / (1.0 + gain)
            lows[f : f + 1, :] = s * gain
            y = (jnp.where(eye, 2.0, 0.0) - mm(shifted[f], x)) * s
            state[f] = mm(x, y)

    count = steps[0, 0].astype(I32)

    @pl.loop(0, count)
    def _(step):
        improve(mm3)

    improve(high)
    for f in range(NF):
        basis[f] = mm3(cross_ref[f], state[f])
        stores.append(pltpu.make_async_copy(basis.at[f], basis_hbm.at[f], sem.at[2 + f]))
        stores[2 + f].start()
    for store in stores:
        store.wait()


def body(front, omega, child_sketch, child_map, picks):
    child = child_sketch.reshape(NF, 32, R)
    any_space = pl.BlockSpec(memory_space=pltpu.HBM)
    vmem = pl.BlockSpec(memory_space=pltpu.VMEM)
    dma = pltpu.SemaphoreType.DMA
    exchanged = pl.pallas_call(
        exchange_kernel,
        out_shape=(
            jax.ShapeDtypeStruct((NF, K, K), F32),
            jax.ShapeDtypeStruct((NF, LB, K), F32),
            jax.ShapeDtypeStruct((NF, 32, LB), F32),
            jax.ShapeDtypeStruct((8, 128), F32),
            jax.ShapeDtypeStruct((NF, K, 2 * K), BF16),
        ),
        in_specs=[any_space] * 5,
        out_specs=(vmem,) * 5,
        scratch_shapes=[
            pltpu.VMEM((NF, LB, 1024), BF16),
            pltpu.VMEM((NF, 1024, R), BF16),
            pltpu.VMEM((NF, 2, NZ, 32, R), BF16),
            pltpu.VMEM((2, NZ, 8, 128), I32),
            pltpu.VMEM((NF, 2, 16), I32),
            pltpu.VMEM((NF, 16, K), I32),
            pltpu.VMEM((NF, LB, R), F32),
            pltpu.VMEM((NF, NC, SLOT, 128), I32),
            pltpu.VMEM((NF, NC, SLOT, 128), I32),
            pltpu.VMEM((NF, NC, SLOT, 128), I32),
            pltpu.VMEM((16, 8, 128), F32),
            pltpu.VMEM((NC, 8, 128), F32),
            pltpu.VMEM((NF, K, LB), BF16),
            pltpu.VMEM((LB, R), BF16),
            pltpu.VMEM((LB, R), BF16),
            pltpu.VMEM((LB, 128), F32),
            dma((11,)),
            dma((NF, 7)), dma((NF, NZ)),
            dma((8,)), dma((9,)),
            dma((NF,)), dma((NF,)),
            dma((NF, 7)), dma((NF, NC)),
            dma((NF, 7)), dma((NF, NC)),
            dma((15,)), dma((16,)),
            dma((7,)), dma((NC,)),
        ],
        compiler_params=pltpu.CompilerParams(
            collective_id=0, has_side_effects=True, vmem_limit_bytes=48 * 2**20
        ),
        name="exchange",
    )(*(pltpu.with_memory_space_constraint(x, pltpu.HBM) for x in (front, omega, child, child_map, picks)))
    own, basis, coupling = pl.pallas_call(
        solve_kernel,
        out_shape=(
            jax.ShapeDtypeStruct((NF, 32, LB), F32),
            jax.ShapeDtypeStruct((NF, LB, K), F32),
            jax.ShapeDtypeStruct((NF, K, 2 * K), BF16),
        ),
        in_specs=[vmem] * 5,
        out_specs=(any_space,) * 3,
        scratch_shapes=[
            pltpu.VMEM((NF, K, K), F32),
            pltpu.VMEM((NF, K, K), F32),
            pltpu.VMEM((8, K), F32),
            pltpu.VMEM((NF, LB, K), F32),
            dma((5,)),
        ],
        compiler_params=pltpu.CompilerParams(vmem_limit_bytes=48 * 2**20),
        name="solve",
    )(*exchanged)
    return jnp.transpose(own, (0, 2, 1)), basis, coupling


def solution(mesh):
    return jax.shard_map(
        body,
        mesh=mesh,
        in_specs=(
            P("fr", "gr", "gc"),
            P("fr", "gc", None),
            P("fr", None, ("gr", "gc"), None),
            P("fr", None, ("gr", "gc")),
            P("fr", None, None),
        ),
        out_specs=(P("fr", "gr", "gc"), P("fr", "gr", None), P("fr", "gr", "gc")),
        check_vma=False,
    )
```
